256 devices in a mesh: wide: 32 (over x, z_lo, y), narrow: 8 (over z_hi, core).
Axes of the slice: x: 4, y: 4, z: 8 (z_hi: 4, z_lo: 2; z = z_hi * 2 + z_lo), core: 2. Of those that a mesh axis runs over, the one named last changes fastest.
Arguments:
- volume: bfloat16 [1, 8, 128, 1024], P(None, None, 'wide', 'narrow'), may hold values from -6 to 6
- w_enter: bfloat16 [27, 32, 1], replicated, may hold values from -1.25 to 1.25
- gain_enter: float32 [32], replicated, may hold values from 0.25 to 1.75
- shift_enter: float32 [32], replicated, may hold values from -2.5 to 2.5
- w_encode: bfloat16 [27, 32, 32], replicated, may hold values from -0.21875 to 0.21875
- gain_encode: float32 [32], replicated, may hold values from 0.25 to 1.75
- shift_encode: float32 [32], replicated, may hold values from -2.5 to 2.5
- w_widen: bfloat16 [27, 64, 32], replicated, may hold values from -0.21875 to 0.21875
- gain_widen: float32 [64], replicated, may hold values from 0.25 to 1.75
- shift_widen: float32 [64], replicated, may hold values from -2.5 to 2.5
- w_deep: bfloat16 [27, 64, 64], replicated, may hold values from -0.15625 to 0.15625
- gain_deep: float32 [64], replicated, may hold values from 0.25 to 1.75
- shift_deep: float32 [64], replicated, may hold values from -2.5 to 2.5
- w_upward: bfloat16 [8, 32, 64], replicated, may hold values from -0.75 to 0.75
- w_decode: bfloat16 [27, 32, 64], replicated, may hold values from -0.15625 to 0.15625
- gain_decode: float32 [32], replicated, may hold values from 0.25 to 1.75
- shift_decode: float32 [32], replicated, may hold values from -2.5 to 2.5
- w_classes: bfloat16 [2, 32], replicated, may hold values from -1 to 1
- bias_classes: float32 [2], replicated, may hold values from -2.5 to 2.5
Outputs:
- logits: float32 [2, 8, 128, 1024], P(None, None, 'wide', 'narrow')
The draws below stay inside these ranges and needn't reach their ends.
All inputs are finite; a program needn't handle non-finite values.
Results may differ from the reference program's by a relative error of at most 0.0054.
Values may be sent and summed in bfloat16 or wider, within the bound.
A program may use at most 64 MiB of HBM per device.

```python
import jax
import jax.numpy as jnp
from jax import lax

BASE = 32
DEEP = 64
CLASSES = 2
DEPTH = 8
NY = 128
NX = 1024


def levels(stream_key, shape, split, low, high):
    factor_of = 1.0
    for dim, parts in split:
        steps = jax.random.uniform(jax.random.fold_in(jax.random.fold_in(stream_key, 6), dim), (parts,), jnp.float32, low / len(split), high / len(split))
        factor_of = factor_of * jnp.repeat(jnp.exp(steps), shape[dim] // parts).reshape((-1,) + (1,) * (len(shape) - 1 - dim))
    return factor_of


def gaussian(key, shape, spread, bound, shards=(), held_as=jnp.bfloat16):
    array = jax.random.normal(key, shape, jnp.float32) * spread
    if len(shards) > 0:
        array = levels(key, shape, shards, -0.22, 0.18) * array
    return jnp.clip(array, min=-bound, max=bound).astype(held_as)


def setup_inputs(seed: int = 0) -> dict:
    keys = jax.random.split(jax.random.key(seed), 20)
    return {
        "volume": gaussian(keys[0], (1, DEPTH, NY, NX), 1.0, 6.0, ((2, 32), (3, 8))),
        "w_enter": gaussian(keys[1], (27, BASE, 1), 27 ** -0.5, 1.25),
        "gain_enter": jnp.clip(1.0 + 0.15 * jax.random.normal(keys[2], (BASE,), jnp.float32), 0.25, 1.75),
        "shift_enter": gaussian(keys[3], (BASE,), 0.3, 2.5, (), jnp.float32),
        "w_encode": gaussian(keys[4], (27, BASE, BASE), (27 * BASE) ** -0.5, 0.21875),
        "gain_encode": jnp.clip(1.0 + 0.15 * jax.random.normal(keys[5], (BASE,), jnp.float32), 0.25, 1.75),
        "shift_encode": gaussian(keys[6], (BASE,), 0.3, 2.5, (), jnp.float32),
        "w_widen": gaussian(keys[7], (27, DEEP, BASE), (27 * BASE) ** -0.5, 0.21875),
        "gain_widen": jnp.clip(1.0 + 0.15 * jax.random.normal(keys[8], (DEEP,), jnp.float32), 0.25, 1.75),
        "shift_widen": gaussian(keys[9], (DEEP,), 0.3, 2.5, (), jnp.float32),
        "w_deep": gaussian(keys[10], (27, DEEP, DEEP), (27 * DEEP) ** -0.5, 0.15625),
        "gain_deep": jnp.clip(1.0 + 0.15 * jax.random.normal(keys[11], (DEEP,), jnp.float32), 0.25, 1.75),
        "shift_deep": gaussian(keys[12], (DEEP,), 0.3, 2.5, (), jnp.float32),
        "w_upward": gaussian(keys[13], (8, BASE, DEEP), DEEP ** -0.5, 0.75),
        "w_decode": gaussian(keys[14], (27, BASE, 2 * BASE), (54 * BASE) ** -0.5, 0.15625),
        "gain_decode": jnp.clip(1.0 + 0.15 * jax.random.normal(keys[15], (BASE,), jnp.float32), 0.25, 1.75),
        "shift_decode": gaussian(keys[16], (BASE,), 0.3, 2.5, (), jnp.float32),
        "w_classes": gaussian(keys[17], (CLASSES, BASE), BASE ** -0.5, 1.0),
        "bias_classes": gaussian(keys[18], (CLASSES,), 0.5, 2.5, (), jnp.float32),
    }


def conv_layer(source, kernel, gain, offset):
    padded = jnp.pad(source, ((0, 0), (1, 1), (1, 1), (1, 1)))
    row_count = source.shape[2]
    col_count = source.shape[3]
    kernel_wide = kernel.astype(jnp.float32)

    def one_plane(plane_index):
        window = lax.dynamic_slice_in_dim(padded, plane_index, 3, 1).astype(jnp.float32)
        total = jnp.zeros((kernel.shape[1], row_count, col_count), jnp.float32)
        for depth_step in range(3):
            for row_step in range(3):
                for col_step in range(3):
                    tap_weight = kernel_wide[9 * depth_step + 3 * row_step + col_step]
                    piece = window[:, depth_step, row_step:row_step + row_count, col_step:col_step + col_count]
                    total = total + jnp.einsum("oc,cyx->oyx", tap_weight, piece)
        return total

    planes = lax.map(one_plane, jnp.arange(source.shape[1], dtype=jnp.int32))
    summed = jnp.transpose(planes, (1, 0, 2, 3))
    return jax.nn.relu(gain[:, None, None, None] * summed + offset[:, None, None, None]).astype(jnp.bfloat16)


def pool_max(source):
    shape_in = source.shape
    blocks = source.reshape(shape_in[0], shape_in[1] // 2, 2, shape_in[2] // 2, 2, shape_in[3] // 2, 2)
    return jnp.max(blocks, axis=(2, 4, 6))


def up_sample(coarse, kernel):
    taps = jnp.einsum("koc,czyx->kozyx", kernel.astype(jnp.float32), coarse.astype(jnp.float32))
    out_ch = kernel.shape[1]
    shape_in = coarse.shape
    taps = taps.reshape(2, 2, 2, out_ch, shape_in[1], shape_in[2], shape_in[3])
    taps = jnp.transpose(taps, (3, 4, 0, 5, 1, 6, 2))
    return taps.reshape(out_ch, 2 * shape_in[1], 2 * shape_in[2], 2 * shape_in[3]).astype(jnp.bfloat16)


def reference(volume, w_enter, gain_enter, shift_enter, w_encode, gain_encode, shift_encode, w_widen, gain_widen, shift_widen, w_deep, gain_deep, shift_deep, w_upward, w_decode, gain_decode, shift_decode, w_classes, bias_classes):
    first = conv_layer(volume, w_enter, gain_enter, shift_enter)
    skip = conv_layer(first, w_encode, gain_encode, shift_encode)
    pooled = pool_max(skip)
    widened = conv_layer(pooled, w_widen, gain_widen, shift_widen)
    deepest = conv_layer(widened, w_deep, gain_deep, shift_deep)
    lifted = up_sample(deepest, w_upward)
    joined = jnp.concatenate([skip, lifted], axis=0)
    decoded = conv_layer(joined, w_decode, gain_decode, shift_decode)
    scores = jnp.einsum("kc,czyx->kzyx", w_classes.astype(jnp.float32), decoded.astype(jnp.float32))
    return scores + bias_classes[:, None, None, None]
```

```python
import functools

import jax
import jax.numpy as jnp
from jax import lax
from jax.experimental import pallas as pl
from jax.experimental.pallas import tpu as pltpu
from jax.sharding import PartitionSpec as P

F32 = jnp.float32
BF16 = jnp.bfloat16
MESH = pl.DeviceIdType.MESH

DEPTH = 8
ROWS = 4
COLS = 128
HALF = 64
XC = 80
OFFSETS = [
    (dy, dx) for dy in (-2, 2, -1, 1, 0) for dx in (-1, 1, 0) if (dy, dx) != (0, 0)
]
POOL_PLANE = (0, 2, 1, 3)


def iota(shape, dim):
    return lax.broadcasted_iota(jnp.int32, shape, dim)


def dot(a, b):
    return jnp.dot(a, b, preferred_element_type=F32)


def dot_nt(a, b):
    return lax.dot_general(a, b, (((1,), (1,)), ((), ())), preferred_element_type=F32)


def eye(n):
    return (iota((n, n), 0) == iota((n, n), 1)).astype(BF16)


def repeat_matrix(n, total, dtype):
    return (iota((n, total), 0) == lax.rem(iota((n, total), 1), n)).astype(dtype)


def band(lane, width, tile, plane, taps):
    group = lane // width
    first = plane - tile * (128 // width)
    out = jnp.zeros(taps[0].shape, F32)
    for dz in range(3):
        place = first + 1 - dz
        if 0 <= place < 128 // width:
            out = jnp.where(group == place, taps[dz], out)
    return out


def kernel(
    n_wide,
    n_narrow,
    volume,
    w_enter,
    w_encode,
    w_widen,
    w_deep,
    w_upward,
    w_decode,
    w_classes,
    gain_enter,
    shift_enter,
    gain_encode,
    shift_encode,
    gain_widen,
    shift_widen,
    gain_deep,
    shift_deep,
    gain_decode,
    shift_decode,
    bias,
    out,
    v_volume,
    v_enter,
    v_encode,
    v_widen,
    v_deep,
    v_upward,
    v_decode,
    v_classes,
    v_gain_enter,
    v_shift_enter,
    v_gain_encode,
    v_shift_encode,
    v_gain_widen,
    v_shift_widen,
    v_gain_deep,
    v_shift_deep,
    v_gain_decode,
    v_shift_decode,
    s_bias,
    plane_rows,
    own,
    halo,
    m_enter,
    m_encode,
    m_widen,
    m_deep,
    m_upward,
    m_decode,
    first,
    skip,
    pooled,
    widened,
    lifted,
    decoded,
    load_sem,
    send_sem,
    recv_sem,
):
    w = lax.axis_index("wide")
    n = lax.axis_index("narrow")

    def partner(offset):
        return (
            lax.rem(w + offset[0] + n_wide, n_wide),
            lax.rem(n + offset[1] + n_narrow, n_narrow),
        )

    barrier = pltpu.get_barrier_semaphore()
    for offset in OFFSETS:
        pl.semaphore_signal(barrier, inc=1, device_id=partner(offset), device_id_type=MESH)

    sources = (
        volume, w_enter, w_encode, w_widen, w_deep, w_upward, w_decode, w_classes,
        gain_enter, shift_enter, gain_encode, shift_encode, gain_widen, shift_widen,
        gain_deep, shift_deep, gain_decode, shift_decode, bias,
    )
    targets = (
        v_volume, v_enter, v_encode, v_widen, v_deep, v_upward, v_decode, v_classes,
        v_gain_enter, v_shift_enter, v_gain_encode, v_shift_encode, v_gain_widen, v_shift_widen,
        v_gain_deep, v_shift_deep, v_gain_decode, v_shift_decode, s_bias,
    )
    loads = [
        pltpu.make_async_copy(source, target, load_sem.at[k])
        for k, (source, target) in enumerate(zip(sources, targets))
    ]
    for load in loads:
        load.start()

    loads[0].wait()
    for z in range(DEPTH):
        plane_rows[ROWS * z : ROWS * (z + 1), :] = v_volume[z].astype(F32)
    by_row = jnp.concatenate(
        [plane_rows[pl.ds(y, DEPTH, stride=ROWS), :] for y in range(ROWS)], axis=0
    )
    by_row = pltpu.roll(by_row, HALF, 1).astype(BF16)
    own[...] = by_row
    halo[1, 64:96, :] = by_row

    pl.semaphore_wait(barrier, len(OFFSETS))
    sends = []
    for k, offset in enumerate(OFFSETS):
        send = pltpu.make_async_remote_copy(
            src_ref=own,
            dst_ref=halo.at[1 - offset[1], pl.ds(32 * (2 - offset[0]), 32)],
            send_sem=send_sem.at[k],
            recv_sem=recv_sem.at[k],
            device_id=partner(offset),
            device_id_type=MESH,
        )
        send.start()
        sends.append(send)

    for load in loads[1:]:
        load.wait()

    def rows_of(refs):
        return jnp.concatenate([ref[...].reshape(1, ref.shape[0]) for ref in refs], axis=0)

    fine = jnp.dot(
        rows_of((v_gain_enter, v_shift_enter, v_gain_encode, v_shift_encode, v_gain_decode, v_shift_decode)),
        repeat_matrix(32, 256, F32),
        preferred_element_type=F32,
        precision=lax.Precision.HIGHEST,
    )
    coarse = jnp.dot(
        rows_of((v_gain_widen, v_shift_widen, v_gain_deep, v_shift_deep)),
        repeat_matrix(64, 256, F32),
        preferred_element_type=F32,
        precision=lax.Precision.HIGHEST,
    )

    taps = dot(v_enter[...], repeat_matrix(32, 256, BF16))
    offset_of = iota((DEPTH, 256), 0) - iota((DEPTH, 256), 1) // 32 + 1
    zero = jnp.zeros((DEPTH, 256), F32)
    blocks = {}
    for dx in range(3):
        for dy in range(3):
            block = zero
            for dz in range(3):
                row = 9 * dz + 3 * dy + dx
                block = jnp.where(
                    offset_of == dz, jnp.broadcast_to(taps[row : row + 1], (DEPTH, 256)), block
                )
            blocks[dx, dy] = block
    for yo in range(6):
        for px in range(2):
            pieces = [
                blocks.get((s - px, yin - yo), zero) for s in range(4) for yin in range(8)
            ]
            m_enter[yo, px] = jnp.concatenate(pieces, axis=0).astype(BF16)

    eye32 = eye(32)
    eye64 = eye(64)
    lane32 = iota((32, 128), 1)
    lane64 = iota((64, 128), 1)

    def build_fine(tap, carry):
        rows = [v_encode[9 * dz + tap] for dz in range(3) for _ in range(4)]
        turned = dot_nt(eye32, jnp.concatenate(rows, axis=0))
        parts = [turned[:, 128 * dz : 128 * (dz + 1)] for dz in range(3)]
        for z in range(DEPTH):
            for tile in range(2):
                m_encode[tap, 32 * z : 32 * (z + 1), 128 * tile : 128 * (tile + 1)] = band(
                    lane32, 32, tile, z, parts
                ).astype(BF16)
        rows = [v_decode[9 * dz + tap] for dz in range(3) for _ in range(4)]
        turned = dot_nt(eye64, jnp.concatenate(rows, axis=0))
        for source in range(2):
            parts = [
                turned[32 * source : 32 * (source + 1), 128 * dz : 128 * (dz + 1)]
                for dz in range(3)
            ]
            for z in range(DEPTH):
                for tile in range(2):
                    m_decode[
                        tap, source, 32 * z : 32 * (z + 1), 128 * tile : 128 * (tile + 1)
                    ] = band(lane32, 32, tile, z, parts).astype(BF16)
        return carry

    lax.fori_loop(0, 9, build_fine, 0)

    repeat64 = repeat_matrix(64, 128, BF16)

    def build_coarse(tap, carry):
        rows = [v_widen[9 * dz + tap] for dz in range(3)]
        turned = dot(jnp.concatenate(rows, axis=0), repeat64)
        parts = [turned[32 * dz : 32 * (dz + 1)] for dz in range(3)]
        for group in range(4):
            for tile in range(2):
                m_widen[tap, 32 * group : 32 * (group + 1), 128 * tile : 128 * (tile + 1)] = band(
                    lane32, 64, tile, POOL_PLANE[group], parts
                ).astype(BF16)
        rows = [v_deep[9 * dz + tap] for dz in range(3) for _ in range(2)]
        turned = dot_nt(eye64, jnp.concatenate(rows, axis=0))
        parts = [turned[:, 128 * dz : 128 * (dz + 1)] for dz in range(3)]
        for z in range(4):
            for tile in range(2):
                m_deep[tap, 64 * z : 64 * (z + 1), 128 * tile : 128 * (tile + 1)] = band(
                    lane64, 64, tile, z, parts
                ).astype(BF16)
        return carry

    lax.fori_loop(0, 9, build_coarse, 0)

    def build_upward(tap, carry):
        rows = [v_upward[4 * a + tap] for _ in range(2) for a in range(2)]
        turned = dot_nt(eye64, jnp.concatenate(rows, axis=0))
        for z in range(4):
            for tile in range(2):
                m_upward[tap, 64 * z : 64 * (z + 1), 128 * tile : 128 * (tile + 1)] = jnp.where(
                    lane64 // 64 == z - 2 * tile, turned, 0.0
                ).astype(BF16)
        return carry

    lax.fori_loop(0, 4, build_upward, 0)

    classes = dot(v_classes[...], repeat_matrix(32, 256, BF16))
    at_row = iota((64, 256), 0)
    at_lane = iota((64, 256), 1)
    per_class = jnp.where(
        at_row < 32,
        jnp.broadcast_to(classes[0:1], (64, 256)),
        jnp.broadcast_to(classes[1:2], (64, 256)),
    )
    per_plane = jnp.where(lax.rem(at_row, 32) // 4 == at_lane // 32, per_class, 0.0)
    m_classes = jnp.concatenate(
        [jnp.where(lax.rem(at_row, 4) == y, per_plane, 0.0) for y in range(ROWS)], axis=1
    ).astype(BF16)

    def inside(at, count):
        return jnp.logical_and(at >= 0, at < count).astype(F32)

    left = inside(n - 1, n_narrow)
    right = inside(n + 1, n_narrow)

    def relu_inside(acc, gain, shift, keep):
        gain = gain * keep
        shift = shift * keep
        return jnp.concatenate(
            [
                jnp.maximum(acc[0:64] * gain + shift, 0.0),
                jnp.maximum(acc[64:72] * (gain * right) + shift * right, 0.0),
                jnp.maximum(acc[72:80] * (gain * left) + shift * left, 0.0),
            ],
            axis=0,
        )

    def put_columns(ref, row, parity, value):
        ref[1 + parity, row] = value.astype(BF16)
        if parity == 0:
            ref[3, row] = pltpu.roll(value, XC - 1, 0).astype(BF16)
        else:
            ref[0, row] = pltpu.roll(value, 1, 0).astype(BF16)

    for send in sends:
        send.wait()

    lane = iota((32, 128), 1)
    wide_rows = []
    for block in range(5):
        keep = inside(w + block - 2, n_wide)
        rows = pl.ds(32 * block, 32)
        middle = halo[1, rows, :].astype(F32) * keep
        before = halo[0, rows, :].astype(F32) * (keep * left)
        after = halo[2, rows, :].astype(F32) * (keep * right)
        wide_rows.append(
            jnp.concatenate(
                [jnp.where(lane < HALF, before, middle), jnp.where(lane < HALF, middle, after)],
                axis=1,
            )
        )
    wide_rows = jnp.concatenate(wide_rows, axis=0)
    shifted = [
        (wide_rows if s == 1 else pltpu.roll(wide_rows, (1 - s) % 256, 1)).astype(BF16)
        for s in range(4)
    ]
    at = iota((XC, 256), 0)
    pick = (
        iota((XC, 256), 1) == 2 * jnp.where(at < 72, at, at - XC) + HALF
    ).astype(BF16)
    columns = jnp.concatenate(
        [
            dot_nt(
                pick, jnp.concatenate([piece[48 * g : 48 * g + 64] for piece in shifted], axis=0)
            ).astype(BF16)
            for g in range(3)
        ],
        axis=0,
    )

    for yo in range(6):
        for px in range(2):
            acc = dot(columns, m_enter[yo, px])
            for g in range(3):
                row = 6 * g + yo
                keep = inside(w * ROWS - 7 + row, n_wide * ROWS)
                put_columns(
                    first, row, px,
                    relu_inside(acc[XC * g : XC * (g + 1)], fine[0:1], fine[1:2], keep),
                )

    matrix = m_encode[...].reshape(9 * 256, 256)
    parity_acc = []
    for px in range(2):
        pieces = [
            first[px + dx, dy : dy + 16].reshape(16 * XC, 256)
            for dy in range(3)
            for dx in range(3)
        ]
        parity_acc.append(dot(jnp.concatenate(pieces, axis=1), matrix))
    pool_lane = lax.rem(iota((XC, 128), 1), 64) < 32
    for k in range(8):
        keep = inside(w * 2 - 3 + k, n_wide * 2)
        best = None
        for y in range(2):
            row = 2 * k + y
            for px in range(2):
                value = relu_inside(
                    parity_acc[px][XC * row : XC * (row + 1)], fine[2:3], fine[3:4], keep
                )
                if 5 <= row <= 10:
                    put_columns(skip, row - 5, px, value)
                best = value if best is None else jnp.maximum(best, value)
        low = best[:, 0:128]
        high = best[:, 128:256]
        low = jnp.maximum(low, pltpu.roll(low, 96, 1))
        high = jnp.maximum(high, pltpu.roll(high, 96, 1))
        best = jnp.where(pool_lane, low, pltpu.roll(high, 32, 1))
        pooled[0, k] = pltpu.roll(best, 1, 0).astype(BF16)
        pooled[1, k] = best.astype(BF16)
        pooled[2, k] = pltpu.roll(best, XC - 1, 0).astype(BF16)

    pieces = [
        pooled[dx, dy : dy + 6].reshape(6 * XC, 128) for dy in range(3) for dx in range(3)
    ]
    acc = dot(jnp.concatenate(pieces, axis=1), m_widen[...].reshape(9 * 128, 256))
    for k in range(6):
        keep = inside(w * 2 - 2 + k, n_wide * 2)
        value = relu_inside(acc[XC * k : XC * (k + 1)], coarse[0:1], coarse[1:2], keep)
        widened[0, k] = pltpu.roll(value, 1, 0).astype(BF16)
        widened[1, k] = value.astype(BF16)
        widened[2, k] = pltpu.roll(value, XC - 1, 0).astype(BF16)

    pieces = [
        widened[dx, dy : dy + 4].reshape(4 * XC, 256) for dy in range(3) for dx in range(3)
    ]
    acc = dot(jnp.concatenate(pieces, axis=1), m_deep[...].reshape(9 * 256, 256))
    deepest = jnp.concatenate(
        [
            relu_inside(
                acc[XC * k : XC * (k + 1)],
                coarse[2:3],
                coarse[3:4],
                inside(w * 2 - 1 + k, n_wide * 2),
            )
            for k in range(4)
        ],
        axis=0,
    ).astype(BF16)

    for b in range(2):
        source = deepest[XC * (1 - b) : XC * (4 - b)]
        for e in range(2):
            acc = dot(source, m_upward[2 * b + e])
            for k in range(3):
                put_columns(lifted, 2 * k + 1 - b, e, acc[XC * k : XC * (k + 1)])

    parities = []
    for px in range(2):
        pieces = [
            ref[px + dx, dy : dy + ROWS, 0:HALF].reshape(ROWS * HALF, 256)
            for dy in range(3)
            for dx in range(3)
            for ref in (skip, lifted)
        ]
        parities.append(jnp.concatenate(pieces, axis=1))
    acc = dot(jnp.concatenate(parities, axis=0), m_decode[...].reshape(18 * 256, 256))
    value = jnp.maximum(acc * fine[4:5] + fine[5:6], 0.0)
    for px in range(2):
        for y in range(ROWS):
            start = (px * ROWS + y) * HALF
            for tile in range(2):
                decoded[tile, pl.ds(y * COLS + px, HALF, stride=2), :] = value[
                    start : start + HALF, 128 * tile : 128 * (tile + 1)
                ]

    features = jnp.concatenate(
        [
            decoded[tile, y * COLS : (y + 1) * COLS, :].astype(BF16)
            for y in range(ROWS)
            for tile in range(2)
        ],
        axis=1,
    )
    logits = dot_nt(m_classes, features)
    out[...] = logits + jnp.where(iota((64, 128), 0) < 32, s_bias[0], s_bias[1])


def per_device(
    n_wide,
    n_narrow,
    volume,
    w_enter,
    gain_enter,
    shift_enter,
    w_encode,
    gain_encode,
    shift_encode,
    w_widen,
    gain_widen,
    shift_widen,
    w_deep,
    gain_deep,
    shift_deep,
    w_upward,
    w_decode,
    gain_decode,
    shift_decode,
    w_classes,
    bias_classes,
):
    operands = (
        volume.reshape(DEPTH, ROWS, COLS),
        w_enter.reshape(27, 32),
        w_encode,
        jnp.transpose(w_widen, (0, 2, 1)),
        w_deep,
        w_upward,
        w_decode,
        w_classes,
        gain_enter,
        shift_enter,
        gain_encode,
        shift_encode,
        gain_widen,
        shift_widen,
        gain_deep,
        shift_deep,
        gain_decode,
        shift_decode,
        bias_classes,
    )
    copies = [pltpu.VMEM(x.shape, x.dtype) for x in operands[:-1]]
    copies.append(pltpu.SMEM((2,), F32))
    logits = pl.pallas_call(
        functools.partial(kernel, n_wide, n_narrow),
        out_shape=jax.ShapeDtypeStruct((64, COLS), F32),
        in_specs=[pl.BlockSpec(memory_space=pltpu.HBM)] * len(operands),
        out_specs=pl.BlockSpec(memory_space=pltpu.VMEM),
        scratch_shapes=copies
        + [
            pltpu.VMEM((32, COLS), F32),
            pltpu.VMEM((32, COLS), BF16),
            pltpu.VMEM((3, 160, COLS), BF16),
            pltpu.VMEM((6, 2, 256, 256), BF16),
            pltpu.VMEM((9, 256, 256), BF16),
            pltpu.VMEM((9, 128, 256), BF16),
            pltpu.VMEM((9, 256, 256), BF16),
            pltpu.VMEM((4, 256, 256), BF16),
            pltpu.VMEM((9, 2, 256, 256), BF16),
            pltpu.VMEM((4, 18, XC, 256), BF16),
            pltpu.VMEM((4, 6, XC, 256), BF16),
            pltpu.VMEM((3, 8, XC, 128), BF16),
            pltpu.VMEM((3, 6, XC, 256), BF16),
            pltpu.VMEM((4, 6, XC, 256), BF16),
            pltpu.VMEM((2, ROWS * COLS, 128), F32),
            pltpu.SemaphoreType.DMA((len(operands),)),
            pltpu.SemaphoreType.DMA((len(OFFSETS),)),
            pltpu.SemaphoreType.DMA((len(OFFSETS),)),
        ],
        compiler_params=pltpu.CompilerParams(
            collective_id=0, has_side_effects=True, vmem_limit_bytes=52 * 1024 * 1024
        ),
        name="unet",
    )(*operands)
    return logits.reshape(2, DEPTH, ROWS, COLS)


def solution(mesh):
    in_specs = (P(None, None, "wide", "narrow"),) + (P(),) * 18
    return jax.shard_map(
        functools.partial(per_device, mesh.shape["wide"], mesh.shape["narrow"]),
        mesh=mesh,
        in_specs=in_specs,
        out_specs=P(None, None, "wide", "narrow"),
        check_vma=False,
    )
```

```python
import functools

import jax
import jax.numpy as jnp
from jax import lax
from jax.experimental import pallas as pl
from jax.experimental.pallas import tpu as pltpu
from jax.sharding import PartitionSpec as P

F32 = jnp.float32
BF16 = jnp.bfloat16
MESH = pl.DeviceIdType.MESH

DEPTH = 8
ROWS = 4
COLS = 128
HALF = 64
XC = 80
OFFSETS = [
    (dy, dx) for dy in (-2, 2, -1, 1, 0) for dx in (-1, 1, 0) if (dy, dx) != (0, 0)
]
POOL_PLANE = (0, 2, 1, 3)


def iota(shape, dim):
    return lax.broadcasted_iota(jnp.int32, shape, dim)


def dot(a, b):
    return jnp.dot(a, b, preferred_element_type=F32)


def dot_nt(a, b):
    return lax.dot_general(a, b, (((1,), (1,)), ((), ())), preferred_element_type=F32)


def eye(n):
    return (iota((n, n), 0) == iota((n, n), 1)).astype(BF16)


def repeat_matrix(n, total, dtype):
    return (iota((n, total), 0) == lax.rem(iota((n, total), 1), n)).astype(dtype)


def band(lane, width, tile, plane, taps):
    group = lane // width
    first = plane - tile * (128 // width)
    out = jnp.zeros(taps[0].shape, F32)
    for dz in range(3):
        place = first + 1 - dz
        if 0 <= place < 128 // width:
            out = jnp.where(group == place, taps[dz], out)
    return out


def kernel(
    n_wide,
    n_narrow,
    volume,
    w_enter,
    w_encode,
    w_widen,
    w_deep,
    w_upward,
    w_decode,
    w_classes,
    gain_enter,
    shift_enter,
    gain_encode,
    shift_encode,
    gain_widen,
    shift_widen,
    gain_deep,
    shift_deep,
    gain_decode,
    shift_decode,
    bias,
    out,
    v_volume,
    v_enter,
    v_encode,
    v_widen,
    v_deep,
    v_upward,
    v_decode,
    v_classes,
    v_gain_enter,
    v_shift_enter,
    v_gain_encode,
    v_shift_encode,
    v_gain_widen,
    v_shift_widen,
    v_gain_deep,
    v_shift_deep,
    v_gain_decode,
    v_shift_decode,
    s_bias,
    plane_rows,
    own,
    halo,
    m_enter,
    m_encode,
    m_widen,
    m_deep,
    m_upward,
    m_decode,
    first,
    skip,
    pooled,
    widened,
    lifted,
    decoded,
    load_sem,
    send_sem,
    recv_sem,
):
    w = lax.axis_index("wide")
    n = lax.axis_index("narrow")

    def partner(offset):
        return (
            lax.rem(w + offset[0] + n_wide, n_wide),
            lax.rem(n + offset[1] + n_narrow, n_narrow),
        )

    barrier = pltpu.get_barrier_semaphore()
    for offset in OFFSETS:
        pl.semaphore_signal(barrier, inc=1, device_id=partner(offset), device_id_type=MESH)

    sources = (
        volume, w_enter, w_encode, w_widen, w_deep, w_upward, w_decode, w_classes,
        gain_enter, shift_enter, gain_encode, shift_encode, gain_widen, shift_widen,
        gain_deep, shift_deep, gain_decode, shift_decode, bias,
    )
    targets = (
        v_volume, v_enter, v_encode, v_widen, v_deep, v_upward, v_decode, v_classes,
        v_gain_enter, v_shift_enter, v_gain_encode, v_shift_encode, v_gain_widen, v_shift_widen,
        v_gain_deep, v_shift_deep, v_gain_decode, v_shift_decode, s_bias,
    )
    loads = [
        pltpu.make_async_copy(source, target, load_sem.at[k])
        for k, (source, target) in enumerate(zip(sources, targets))
    ]
    for load in loads:
        load.start()

    loads[0].wait()
    for z in range(DEPTH):
        plane_rows[ROWS * z : ROWS * (z + 1), :] = v_volume[z].astype(F32)
    by_row = jnp.concatenate(
        [plane_rows[pl.ds(y, DEPTH, stride=ROWS), :] for y in range(ROWS)], axis=0
    )
    by_row = pltpu.roll(by_row, HALF, 1).astype(BF16)
    own[...] = by_row
    halo[1, 64:96, :] = by_row

    pl.semaphore_wait(barrier, len(OFFSETS))
    sends = []
    for k, offset in enumerate(OFFSETS):
        send = pltpu.make_async_remote_copy(
            src_ref=own,
            dst_ref=halo.at[1 - offset[1], pl.ds(32 * (2 - offset[0]), 32)],
            send_sem=send_sem.at[k],
            recv_sem=recv_sem.at[k],
            device_id=partner(offset),
            device_id_type=MESH,
        )
        send.start()
        sends.append(send)

    for load in loads[1:]:
        load.wait()

    def rows_of(refs):
        return jnp.concatenate([ref[...].reshape(1, ref.shape[0]) for ref in refs], axis=0)

    fine = jnp.dot(
        rows_of((v_gain_enter, v_shift_enter, v_gain_encode, v_shift_encode, v_gain_decode, v_shift_decode)),
        repeat_matrix(32, 256, F32),
        preferred_element_type=F32,
        precision=lax.Precision.HIGHEST,
    )
    coarse = jnp.dot(
        rows_of((v_gain_widen, v_shift_widen, v_gain_deep, v_shift_deep)),
        repeat_matrix(64, 256, F32),
        preferred_element_type=F32,
        precision=lax.Precision.HIGHEST,
    )

    taps = dot(v_enter[...], repeat_matrix(32, 256, BF16))
    offset_of = iota((DEPTH, 256), 0) - iota((DEPTH, 256), 1) // 32 + 1
    zero = jnp.zeros((DEPTH, 256), F32)
    blocks = {}
    for dx in range(3):
        for dy in range(3):
            block = zero
            for dz in range(3):
                row = 9 * dz + 3 * dy + dx
                block = jnp.where(
                    offset_of == dz, jnp.broadcast_to(taps[row : row + 1], (DEPTH, 256)), block
                )
            blocks[dx, dy] = block
    for yo in range(6):
        for px in range(2):
            pieces = [
                blocks.get((s - px, yin - yo), zero) for s in range(4) for yin in range(8)
            ]
            m_enter[yo, px] = jnp.concatenate(pieces, axis=0).astype(BF16)

    eye32 = eye(32)
    eye64 = eye(64)
    lane32 = iota((32, 128), 1)
    lane64 = iota((64, 128), 1)

    def build_fine(tap, carry):
        rows = [v_encode[9 * dz + tap] for dz in range(3) for _ in range(4)]
        turned = dot_nt(eye32, jnp.concatenate(rows, axis=0))
        parts = [turned[:, 128 * dz : 128 * (dz + 1)] for dz in range(3)]
        for z in range(DEPTH):
            for tile in range(2):
                m_encode[tap, 32 * z : 32 * (z + 1), 128 * tile : 128 * (tile + 1)] = band(
                    lane32, 32, tile, z, parts
                ).astype(BF16)
        rows = [v_decode[9 * dz + tap] for dz in range(3) for _ in range(4)]
        turned = dot_nt(eye64, jnp.concatenate(rows, axis=0))
        for source in range(2):
            parts = [
                turned[32 * source : 32 * (source + 1), 128 * dz : 128 * (dz + 1)]
                for dz in range(3)
            ]
            for z in range(DEPTH):
                for tile in range(2):
                    m_decode[
                        tap, source, 32 * z : 32 * (z + 1), 128 * tile : 128 * (tile + 1)
                    ] = band(lane32, 32, tile, z, parts).astype(BF16)
        return carry

    lax.fori_loop(0, 9, build_fine, 0)

    repeat64 = repeat_matrix(64, 128, BF16)

    def build_coarse(tap, carry):
        rows = [v_widen[9 * dz + tap] for dz in range(3)]
        turned = dot(jnp.concatenate(rows, axis=0), repeat64)
        parts = [turned[32 * dz : 32 * (dz + 1)] for dz in range(3)]
        for group in range(4):
            for tile in range(2):
                m_widen[tap, 32 * group : 32 * (group + 1), 128 * tile : 128 * (tile + 1)] = band(
                    lane32, 64, tile, POOL_PLANE[group], parts
                ).astype(BF16)
        rows = [v_deep[9 * dz + tap] for dz in range(3) for _ in range(2)]
        turned = dot_nt(eye64, jnp.concatenate(rows, axis=0))
        parts = [turned[:, 128 * dz : 128 * (dz + 1)] for dz in range(3)]
        for z in range(4):
            for tile in range(2):
                m_deep[tap, 64 * z : 64 * (z + 1), 128 * tile : 128 * (tile + 1)] = band(
                    lane64, 64, tile, z, parts
                ).astype(BF16)
        return carry

    lax.fori_loop(0, 9, build_coarse, 0)

    def build_upward(tap, carry):
        rows = [v_upward[4 * a + tap] for _ in range(2) for a in range(2)]
        turned = dot_nt(eye64, jnp.concatenate(rows, axis=0))
        for z in range(4):
            for tile in range(2):
                m_upward[tap, 64 * z : 64 * (z + 1), 128 * tile : 128 * (tile + 1)] = jnp.where(
                    lane64 // 64 == z - 2 * tile, turned, 0.0
                ).astype(BF16)
        return carry

    lax.fori_loop(0, 4, build_upward, 0)

    classes = dot(v_classes[...], repeat_matrix(32, 256, BF16))
    at_row = iota((64, 256), 0)
    at_lane = iota((64, 256), 1)
    per_class = jnp.where(
        at_row < 32,
        jnp.broadcast_to(classes[0:1], (64, 256)),
        jnp.broadcast_to(classes[1:2], (64, 256)),
    )
    per_plane = jnp.where(lax.rem(at_row, 32) // 4 == at_lane // 32, per_class, 0.0)
    m_classes = jnp.concatenate(
        [jnp.where(lax.rem(at_row, 4) == y, per_plane, 0.0) for y in range(ROWS)], axis=1
    ).astype(BF16)

    def inside(at, count):
        return jnp.logical_and(at >= 0, at < count).astype(F32)

    left = inside(n - 1, n_narrow)
    right = inside(n + 1, n_narrow)

    def relu_inside(acc, gain, shift, keep):
        gain = gain * keep
        shift = shift * keep
        return jnp.concatenate(
            [
                jnp.maximum(acc[0:64] * gain + shift, 0.0),
                jnp.maximum(acc[64:72] * (gain * right) + shift * right, 0.0),
                jnp.maximum(acc[72:80] * (gain * left) + shift * left, 0.0),
            ],
            axis=0,
        )

    def put_columns(ref, row, parity, value):
        ref[1 + parity, row] = value.astype(BF16)
        if parity == 0:
            ref[3, row] = pltpu.roll(value, XC - 1, 0).astype(BF16)
        else:
            ref[0, row] = pltpu.roll(value, 1, 0).astype(BF16)

    for send in sends:
        send.wait()

    lane = iota((32, 128), 1)
    wide_rows = []
    for block in range(5):
        keep = inside(w + block - 2, n_wide)
        rows = pl.ds(32 * block, 32)
        middle = halo[1, rows, :].astype(F32) * keep
        before = halo[0, rows, :].astype(F32) * (keep * left)
        after = halo[2, rows, :].astype(F32) * (keep * right)
        wide_rows.append(
            jnp.concatenate(
                [jnp.where(lane < HALF, before, middle), jnp.where(lane < HALF, middle, after)],
                axis=1,
            )
        )
    wide_rows = jnp.concatenate(wide_rows, axis=0)
    shifted = [
        (wide_rows if s == 1 else pltpu.roll(wide_rows, (1 - s) % 256, 1)).astype(BF16)
        for s in range(4)
    ]
    at = iota((XC, 256), 0)
    pick = (
        iota((XC, 256), 1) == 2 * jnp.where(at < 72, at, at - XC) + HALF
    ).astype(BF16)
    columns = jnp.concatenate(
        [
            dot_nt(
                pick, jnp.concatenate([piece[48 * g : 48 * g + 64] for piece in shifted], axis=0)
            ).astype(BF16)
            for g in range(3)
        ],
        axis=0,
    )

    for yo in range(6):
        for px in range(2):
            acc = dot(columns, m_enter[yo, px])
            for g in range(3):
                row = 6 * g + yo
                keep = inside(w * ROWS - 7 + row, n_wide * ROWS)
                put_columns(
                    first, row, px,
                    relu_inside(acc[XC * g : XC * (g + 1)], fine[0:1], fine[1:2], keep),
                )

    matrix = m_encode[...].reshape(9 * 256, 256)
    parity_acc = []
    for px in range(2):
        pieces = [
            first[px + dx, dy : dy + 16].reshape(16 * XC, 256)
            for dy in range(3)
            for dx in range(3)
        ]
        parity_acc.append(dot(jnp.concatenate(pieces, axis=1), matrix))
    pool_lane = lax.rem(iota((XC, 128), 1), 64) < 32
    for k in range(8):
        keep = inside(w * 2 - 3 + k, n_wide * 2)
        best = None
        for y in range(2):
            row = 2 * k + y
            for px in range(2):
                value = relu_inside(
                    parity_acc[px][XC * row : XC * (row + 1)], fine[2:3], fine[3:4], keep
                )
                if 5 <= row <= 10:
                    put_columns(skip, row - 5, px, value)
                best = value if best is None else jnp.maximum(best, value)
        low = best[:, 0:128]
        high = best[:, 128:256]
        low = jnp.maximum(low, pltpu.roll(low, 96, 1))
        high = jnp.maximum(high, pltpu.roll(high, 96, 1))
        best = jnp.where(pool_lane, low, pltpu.roll(high, 32, 1))
        pooled[0, k] = pltpu.roll(best, 1, 0).astype(BF16)
        pooled[1, k] = best.astype(BF16)
        pooled[2, k] = pltpu.roll(best, XC - 1, 0).astype(BF16)

    pieces = [
        pooled[dx, dy : dy + 6].reshape(6 * XC, 128) for dy in range(3) for dx in range(3)
    ]
    acc = dot(jnp.concatenate(pieces, axis=1), m_widen[...].reshape(9 * 128, 256))
    for k in range(6):
        keep = inside(w * 2 - 2 + k, n_wide * 2)
        value = relu_inside(acc[XC * k : XC * (k + 1)], coarse[0:1], coarse[1:2], keep)
        widened[0, k] = pltpu.roll(value, 1, 0).astype(BF16)
        widened[1, k] = value.astype(BF16)
        widened[2, k] = pltpu.roll(value, XC - 1, 0).astype(BF16)

    pieces = [
        widened[dx, dy : dy + 4].reshape(4 * XC, 256) for dy in range(3) for dx in range(3)
    ]
    acc = dot(jnp.concatenate(pieces, axis=1), m_deep[...].reshape(9 * 256, 256))
    deepest = jnp.concatenate(
        [
            relu_inside(
                acc[XC * k : XC * (k + 1)],
                coarse[2:3],
                coarse[3:4],
                inside(w * 2 - 1 + k, n_wide * 2),
            )
            for k in range(4)
        ],
        axis=0,
    ).astype(BF16)

    for b in range(2):
        source = deepest[XC * (1 - b) : XC * (4 - b)]
        for e in range(2):
            acc = dot(source, m_upward[2 * b + e])
            for k in range(3):
                put_columns(lifted, 2 * k + 1 - b, e, acc[XC * k : XC * (k + 1)])

    parities = []
    for px in range(2):
        pieces = [
            ref[px + dx, dy : dy + ROWS, 0:HALF].reshape(ROWS * HALF, 256)
            for dy in range(3)
            for dx in range(3)
            for ref in (skip, lifted)
        ]
        parities.append(jnp.concatenate(pieces, axis=1))
    acc = dot(jnp.concatenate(parities, axis=0), m_decode[...].reshape(18 * 256, 256))
    value = jnp.maximum(acc * fine[4:5] + fine[5:6], 0.0)
    for px in range(2):
        for y in range(ROWS):
            start = (px * ROWS + y) * HALF
            for tile in range(2):
                decoded[tile, pl.ds(y * COLS + px, HALF, stride=2), :] = value[
                    start : start + HALF, 128 * tile : 128 * (tile + 1)
                ]

    features = jnp.concatenate(
        [
            decoded[tile, y * COLS : (y + 1) * COLS, :].astype(BF16)
            for y in range(ROWS)
            for tile in range(2)
        ],
        axis=1,
    )
    logits = dot_nt(m_classes, features)
    out[...] = logits + jnp.where(iota((64, 128), 0) < 32, s_bias[0], s_bias[1])


def per_device(
    n_wide,
    n_narrow,
    volume,
    w_enter,
    gain_enter,
    shift_enter,
    w_encode,
    gain_encode,
    shift_encode,
    w_widen,
    gain_widen,
    shift_widen,
    w_deep,
    gain_deep,
    shift_deep,
    w_upward,
    w_decode,
    gain_decode,
    shift_decode,
    w_classes,
    bias_classes,
):
    operands = (
        volume.reshape(DEPTH, ROWS, COLS),
        w_enter.reshape(27, 32),
        w_encode,
        jnp.transpose(w_widen, (0, 2, 1)),
        w_deep,
        w_upward,
        w_decode,
        w_classes,
        gain_enter,
        shift_enter,
        gain_encode,
        shift_encode,
        gain_widen,
        shift_widen,
        gain_deep,
        shift_deep,
        gain_decode,
        shift_decode,
        bias_classes,
    )
    copies = [pltpu.VMEM(x.shape, x.dtype) for x in operands[:-1]]
    copies.append(pltpu.SMEM((2,), F32))
    logits = pl.pallas_call(
        functools.partial(kernel, n_wide, n_narrow),
        out_shape=jax.ShapeDtypeStruct((64, COLS), F32),
        in_specs=[pl.BlockSpec(memory_space=pltpu.HBM)] * len(operands),
        out_specs=pl.BlockSpec(memory_space=pltpu.VMEM),
        scratch_shapes=copies
        + [
            pltpu.VMEM((32, COLS), F32),
            pltpu.VMEM((32, COLS), BF16),
            pltpu.VMEM((3, 160, COLS), BF16),
            pltpu.VMEM((6, 2, 256, 256), BF16),
            pltpu.VMEM((9, 256, 256), BF16),
            pltpu.VMEM((9, 128, 256), BF16),
            pltpu.VMEM((9, 256, 256), BF16),
            pltpu.VMEM((4, 256, 256), BF16),
            pltpu.VMEM((9, 2, 256, 256), BF16),
            pltpu.VMEM((4, 18, XC, 256), BF16),
            pltpu.VMEM((4, 6, XC, 256), BF16),
            pltpu.VMEM((3, 8, XC, 128), BF16),
            pltpu.VMEM((3, 6, XC, 256), BF16),
            pltpu.VMEM((4, 6, XC, 256), BF16),
            pltpu.VMEM((2, ROWS * COLS, 128), F32),
            pltpu.SemaphoreType.DMA((len(operands),)),
            pltpu.SemaphoreType.DMA((len(OFFSETS),)),
            pltpu.SemaphoreType.DMA((len(OFFSETS),)),
        ],
        compiler_params=pltpu.CompilerParams(
            collective_id=0, has_side_effects=True, vmem_limit_bytes=52 * 1024 * 1024
        ),
        name="unet",
    )(*[pltpu.with_memory_space_constraint(x, pltpu.HBM) for x in operands])
    return logits.reshape(2, DEPTH, ROWS, COLS)


def solution(mesh):
    in_specs = (P(None, None, "wide", "narrow"),) + (P(),) * 18
    return jax.shard_map(
        functools.partial(per_device, mesh.shape["wide"], mesh.shape["narrow"]),
        mesh=mesh,
        in_specs=in_specs,
        out_specs=P(None, None, "wide", "narrow"),
        check_vma=False,
    )
```

```python
import functools

import jax
import jax.numpy as jnp
from jax import lax
from jax.experimental import pallas as pl
from jax.experimental.pallas import tpu as pltpu
from jax.sharding import PartitionSpec as P

F32 = jnp.float32
BF16 = jnp.bfloat16
MESH = pl.DeviceIdType.MESH

DEPTH = 8
ROWS = 4
COLS = 128
HALF = 64
XC = 80
OFFSETS = [
    (dy, dx) for dy in (-2, 2, -1, 1, 0) for dx in (-1, 1, 0) if (dy, dx) != (0, 0)
]
POOL_PLANE = (0, 2, 1, 3)


def iota(shape, dim):
    return lax.broadcasted_iota(jnp.int32, shape, dim)


def dot(a, b):
    return jnp.dot(a, b, preferred_element_type=F32)


def dot_nt(a, b):
    return lax.dot_general(a, b, (((1,), (1,)), ((), ())), preferred_element_type=F32)


def eye(n):
    return (iota((n, n), 0) == iota((n, n), 1)).astype(BF16)


def repeat_matrix(n, total, dtype):
    return (iota((n, total), 0) == (iota((n, total), 1) & (n - 1))).astype(dtype)


def band(lane, width, tile, plane, taps):
    group = lane >> (width.bit_length() - 1)
    first = plane - tile * (128 // width)
    out = jnp.zeros(taps[0].shape, F32)
    for dz in range(3):
        place = first + 1 - dz
        if 0 <= place < 128 // width:
            out = jnp.where(group == place, taps[dz], out)
    return out


def kernel(
    n_wide,
    n_narrow,
    volume,
    w_enter,
    w_encode,
    w_widen,
    w_deep,
    w_upward,
    w_decode,
    w_classes,
    gain_enter,
    shift_enter,
    gain_encode,
    shift_encode,
    gain_widen,
    shift_widen,
    gain_deep,
    shift_deep,
    gain_decode,
    shift_decode,
    bias,
    out,
    v_volume,
    v_enter,
    v_encode,
    v_widen,
    v_deep,
    v_upward,
    v_decode,
    v_classes,
    v_gain_enter,
    v_shift_enter,
    v_gain_encode,
    v_shift_encode,
    v_gain_widen,
    v_shift_widen,
    v_gain_deep,
    v_shift_deep,
    v_gain_decode,
    v_shift_decode,
    s_bias,
    plane_rows,
    own,
    halo,
    m_enter,
    m_encode,
    m_widen,
    m_deep,
    m_upward,
    m_decode,
    m_classes,
    fine,
    coarse,
    first,
    skip,
    pooled,
    widened,
    lifted,
    decoded,
    load_sem,
    send_sem,
    recv_sem,
):
    w = lax.axis_index("wide")
    n = lax.axis_index("narrow")

    def within(at, count):
        return jnp.logical_and(at >= 0, at < count)

    def has(dy, dx):
        return jnp.logical_and(within(w + dy, n_wide), within(n + dx, n_narrow))

    halo[...] = jnp.zeros(halo.shape, BF16)

    barrier = pltpu.get_barrier_semaphore()
    for dy, dx in OFFSETS:

        @pl.when(has(dy, dx))
        def _():
            pl.semaphore_signal(
                barrier, inc=1, device_id=(w + dy, n + dx), device_id_type=MESH
            )

    sources = (
        volume, w_enter, w_encode, w_widen, w_deep, w_upward, w_decode, w_classes,
        gain_enter, shift_enter, gain_encode, shift_encode, gain_widen, shift_widen,
        gain_deep, shift_deep, gain_decode, shift_decode, bias,
    )
    targets = (
        v_volume, v_enter, v_encode, v_widen, v_deep, v_upward, v_decode, v_classes,
        v_gain_enter, v_shift_enter, v_gain_encode, v_shift_encode, v_gain_widen, v_shift_widen,
        v_gain_deep, v_shift_deep, v_gain_decode, v_shift_decode, s_bias,
    )
    loads = [
        pltpu.make_async_copy(source, target, load_sem.at[k])
        for k, (source, target) in enumerate(zip(sources, targets))
    ]
    for load in loads:
        load.start()

    loads[0].wait()
    for z in range(DEPTH):
        plane_rows[ROWS * z : ROWS * (z + 1), :] = v_volume[z].astype(F32)
    by_row = jnp.concatenate(
        [plane_rows[pl.ds(y, DEPTH, stride=ROWS), :] for y in range(ROWS)], axis=0
    )
    by_row = pltpu.roll(by_row, HALF, 1).astype(BF16)
    own[...] = by_row
    halo[1, 64:96, :] = by_row

    def exchange(k):
        dy, dx = OFFSETS[k]
        return pltpu.make_async_remote_copy(
            src_ref=own,
            dst_ref=halo.at[1 - dx, pl.ds(32 * (2 - dy), 32)],
            send_sem=send_sem.at[k],
            recv_sem=recv_sem.at[k],
            device_id=(w + dy, n + dx),
            device_id_type=MESH,
        )

    pl.semaphore_wait(barrier, sum(has(dy, dx).astype(jnp.int32) for dy, dx in OFFSETS))
    for k, (dy, dx) in enumerate(OFFSETS):

        @pl.when(has(dy, dx))
        def _():
            exchange(k).start()

    for load in loads[1:]:
        load.wait()

    def rows_of(refs):
        return jnp.concatenate([ref[...].reshape(1, ref.shape[0]) for ref in refs], axis=0)

    fine[...] = jnp.dot(
        rows_of((v_gain_enter, v_shift_enter, v_gain_encode, v_shift_encode, v_gain_decode, v_shift_decode)),
        repeat_matrix(32, 256, F32),
        preferred_element_type=F32,
        precision=lax.Precision.HIGHEST,
    )
    coarse[...] = jnp.dot(
        rows_of((v_gain_widen, v_shift_widen, v_gain_deep, v_shift_deep)),
        repeat_matrix(64, 256, F32),
        preferred_element_type=F32,
        precision=lax.Precision.HIGHEST,
    )

    taps = dot(v_enter[...], repeat_matrix(32, 256, BF16))
    offset_of = iota((DEPTH, 256), 0) - (iota((DEPTH, 256), 1) >> 5) + 1
    zero = jnp.zeros((DEPTH, 256), F32)
    blocks = {}
    for dx in range(3):
        for dy in range(3):
            block = zero
            for dz in range(3):
                row = 9 * dz + 3 * dy + dx
                block = jnp.where(
                    offset_of == dz, jnp.broadcast_to(taps[row : row + 1], (DEPTH, 256)), block
                )
            blocks[dx, dy] = block
    for yo in range(6):
        for px in range(2):
            pieces = [
                blocks.get((s - px, yin - yo), zero) for s in range(4) for yin in range(8)
            ]
            m_enter[yo, px] = jnp.concatenate(pieces, axis=0).astype(BF16)

    eye32 = eye(32)
    eye64 = eye(64)
    lane32 = iota((32, 128), 1)
    lane64 = iota((64, 128), 1)

    def build_fine(tap, carry):
        rows = [v_encode[9 * dz + tap] for dz in range(3) for _ in range(4)]
        turned = dot_nt(eye32, jnp.concatenate(rows, axis=0))
        parts = [turned[:, 128 * dz : 128 * (dz + 1)] for dz in range(3)]
        for z in range(DEPTH):
            for tile in range(2):
                m_encode[tap, 32 * z : 32 * (z + 1), 128 * tile : 128 * (tile + 1)] = band(
                    lane32, 32, tile, z, parts
                ).astype(BF16)
        rows = [v_decode[9 * dz + tap] for dz in range(3) for _ in range(4)]
        turned = dot_nt(eye64, jnp.concatenate(rows, axis=0))
        for source in range(2):
            parts = [
                turned[32 * source : 32 * (source + 1), 128 * dz : 128 * (dz + 1)]
                for dz in range(3)
            ]
            for z in range(DEPTH):
                for tile in range(2):
                    m_decode[
                        tap, source, 32 * z : 32 * (z + 1), 128 * tile : 128 * (tile + 1)
                    ] = band(lane32, 32, tile, z, parts).astype(BF16)
        return carry

    lax.fori_loop(0, 9, build_fine, 0)

    repeat64 = repeat_matrix(64, 128, BF16)

    def build_coarse(tap, carry):
        rows = [v_widen[9 * dz + tap] for dz in range(3)]
        turned = dot(jnp.concatenate(rows, axis=0), repeat64)
        parts = [turned[32 * dz : 32 * (dz + 1)] for dz in range(3)]
        for group in range(4):
            for tile in range(2):
                m_widen[tap, 32 * group : 32 * (group + 1), 128 * tile : 128 * (tile + 1)] = band(
                    lane32, 64, tile, POOL_PLANE[group], parts
                ).astype(BF16)
        rows = [v_deep[9 * dz + tap] for dz in range(3) for _ in range(2)]
        turned = dot_nt(eye64, jnp.concatenate(rows, axis=0))
        parts = [turned[:, 128 * dz : 128 * (dz + 1)] for dz in range(3)]
        for z in range(4):
            for tile in range(2):
                m_deep[tap, 64 * z : 64 * (z + 1), 128 * tile : 128 * (tile + 1)] = band(
                    lane64, 64, tile, z, parts
                ).astype(BF16)
        return carry

    lax.fori_loop(0, 9, build_coarse, 0)

    def build_upward(tap, carry):
        rows = [v_upward[4 * a + tap] for _ in range(2) for a in range(2)]
        turned = dot_nt(eye64, jnp.concatenate(rows, axis=0))
        for z in range(4):
            for tile in range(2):
                m_upward[tap, 64 * z : 64 * (z + 1), 128 * tile : 128 * (tile + 1)] = jnp.where(
                    (lane64 >> 6) == z - 2 * tile, turned, 0.0
                ).astype(BF16)
        return carry

    lax.fori_loop(0, 4, build_upward, 0)

    classes = dot(v_classes[...], repeat_matrix(32, 256, BF16))
    at_row = iota((64, 256), 0)
    at_lane = iota((64, 256), 1)
    per_class = jnp.where(
        at_row < 32,
        jnp.broadcast_to(classes[0:1], (64, 256)),
        jnp.broadcast_to(classes[1:2], (64, 256)),
    )
    per_plane = jnp.where(((at_row & 31) >> 2) == (at_lane >> 5), per_class, 0.0)
    for y in range(ROWS):
        m_classes[:, 256 * y : 256 * (y + 1)] = jnp.where(
            (at_row & 3) == y, per_plane, 0.0
        ).astype(BF16)

    def inside(at, count):
        return within(at, count).astype(F32)

    left = inside(n - 1, n_narrow)
    right = inside(n + 1, n_narrow)

    def relu_inside(acc, gain, shift, keep):
        gain = gain * keep
        shift = shift * keep
        return jnp.concatenate(
            [
                jnp.maximum(acc[0:64] * gain + shift, 0.0),
                jnp.maximum(acc[64:72] * (gain * right) + shift * right, 0.0),
                jnp.maximum(acc[72:80] * (gain * left) + shift * left, 0.0),
            ],
            axis=0,
        )

    def put_columns(ref, row, parity, value):
        ref[1 + parity, row] = value.astype(BF16)
        if parity == 0:
            ref[3, row] = pltpu.roll(value, XC - 1, 0).astype(BF16)
        else:
            ref[0, row] = pltpu.roll(value, 1, 0).astype(BF16)

    for k, (dy, dx) in enumerate(OFFSETS):

        @pl.when(has(-dy, -dx))
        def _():
            exchange(k).wait_recv()

    lane = iota((32, 128), 1)
    wide_rows = []
    for block in range(5):
        rows = pl.ds(32 * block, 32)
        before, middle, after = [halo[side, rows, :].astype(F32) for side in range(3)]
        wide_rows.append(
            jnp.concatenate(
                [jnp.where(lane < HALF, before, middle), jnp.where(lane < HALF, middle, after)],
                axis=1,
            )
        )
    wide_rows = jnp.concatenate(wide_rows, axis=0)
    shifted = [
        (wide_rows if s == 1 else pltpu.roll(wide_rows, (1 - s) % 256, 1)).astype(BF16)
        for s in range(4)
    ]
    at = iota((XC, 256), 0)
    pick = (
        iota((XC, 256), 1) == 2 * jnp.where(at < 72, at, at - XC) + HALF
    ).astype(BF16)
    columns = jnp.concatenate(
        [
            dot_nt(
                pick, jnp.concatenate([piece[48 * g : 48 * g + 64] for piece in shifted], axis=0)
            ).astype(BF16)
            for g in range(3)
        ],
        axis=0,
    )

    for yo in range(6):
        for px in range(2):
            acc = dot(columns, m_enter[yo, px])
            for g in range(3):
                row = 6 * g + yo
                keep = inside(w * ROWS - 7 + row, n_wide * ROWS)
                put_columns(
                    first, row, px,
                    relu_inside(acc[XC * g : XC * (g + 1)], fine[0:1, :], fine[1:2, :], keep),
                )

    matrix = m_encode[...].reshape(9 * 256, 256)
    parity_acc = []
    for px in range(2):
        pieces = [
            first[px + dx, dy : dy + 16].reshape(16 * XC, 256)
            for dy in range(3)
            for dx in range(3)
        ]
        parity_acc.append(dot(jnp.concatenate(pieces, axis=1), matrix))
    pool_lane = (iota((XC, 128), 1) & 32) == 0
    for k in range(8):
        keep = inside(w * 2 - 3 + k, n_wide * 2)
        best = None
        for y in range(2):
            row = 2 * k + y
            for px in range(2):
                value = relu_inside(
                    parity_acc[px][XC * row : XC * (row + 1)], fine[2:3, :], fine[3:4, :], keep
                )
                if 5 <= row <= 10:
                    put_columns(skip, row - 5, px, value)
                best = value if best is None else jnp.maximum(best, value)
        low = best[:, 0:128]
        high = best[:, 128:256]
        low = jnp.maximum(low, pltpu.roll(low, 96, 1))
        high = jnp.maximum(high, pltpu.roll(high, 96, 1))
        best = jnp.where(pool_lane, low, pltpu.roll(high, 32, 1))
        pooled[0, k] = pltpu.roll(best, 1, 0).astype(BF16)
        pooled[1, k] = best.astype(BF16)
        pooled[2, k] = pltpu.roll(best, XC - 1, 0).astype(BF16)

    pieces = [
        pooled[dx, dy : dy + 6].reshape(6 * XC, 128) for dy in range(3) for dx in range(3)
    ]
    acc = dot(jnp.concatenate(pieces, axis=1), m_widen[...].reshape(9 * 128, 256))
    for k in range(6):
        keep = inside(w * 2 - 2 + k, n_wide * 2)
        value = relu_inside(acc[XC * k : XC * (k + 1)], coarse[0:1, :], coarse[1:2, :], keep)
        widened[0, k] = pltpu.roll(value, 1, 0).astype(BF16)
        widened[1, k] = value.astype(BF16)
        widened[2, k] = pltpu.roll(value, XC - 1, 0).astype(BF16)

    pieces = [
        widened[dx, dy : dy + 4].reshape(4 * XC, 256) for dy in range(3) for dx in range(3)
    ]
    acc = dot(jnp.concatenate(pieces, axis=1), m_deep[...].reshape(9 * 256, 256))
    deepest = jnp.concatenate(
        [
            relu_inside(
                acc[XC * k : XC * (k + 1)],
                coarse[2:3, :],
                coarse[3:4, :],
                inside(w * 2 - 1 + k, n_wide * 2),
            )
            for k in range(4)
        ],
        axis=0,
    ).astype(BF16)

    for b in range(2):
        source = deepest[XC * (1 - b) : XC * (4 - b)]
        for e in range(2):
            acc = dot(source, m_upward[2 * b + e])
            for k in range(3):
                put_columns(lifted, 2 * k + 1 - b, e, acc[XC * k : XC * (k + 1)])

    matrix = m_decode[...].reshape(18 * 256, 256)
    accs = []
    for px in range(2):
        pieces = [
            ref[px + dx, dy : dy + ROWS, 0:HALF].reshape(ROWS * HALF, 256)
            for dy in range(3)
            for dx in range(3)
            for ref in (skip, lifted)
        ]
        accs.append(dot(jnp.concatenate(pieces, axis=1), matrix))
    acc = jnp.concatenate(accs, axis=0)
    value = jnp.maximum(acc * fine[4:5, :] + fine[5:6, :], 0.0)
    for px in range(2):
        for y in range(ROWS):
            start = (px * ROWS + y) * HALF
            for tile in range(2):
                decoded[tile, pl.ds(y * COLS + px, HALF, stride=2), :] = value[
                    start : start + HALF, 128 * tile : 128 * (tile + 1)
                ]

    features = jnp.concatenate(
        [
            decoded[tile, y * COLS : (y + 1) * COLS, :].astype(BF16)
            for y in range(ROWS)
            for tile in range(2)
        ],
        axis=1,
    )
    logits = dot_nt(m_classes[...], features)
    for k, (dy, dx) in enumerate(OFFSETS):

        @pl.when(has(dy, dx))
        def _():
            exchange(k).wait_send()

    out[...] = logits + jnp.where(iota((64, 128), 0) < 32, s_bias[0], s_bias[1])


def per_device(
    n_wide,
    n_narrow,
    volume,
    w_enter,
    gain_enter,
    shift_enter,
    w_encode,
    gain_encode,
    shift_encode,
    w_widen,
    gain_widen,
    shift_widen,
    w_deep,
    gain_deep,
    shift_deep,
    w_upward,
    w_decode,
    gain_decode,
    shift_decode,
    w_classes,
    bias_classes,
):
    operands = (
        volume.reshape(DEPTH, ROWS, COLS),
        w_enter.reshape(27, 32),
        w_encode,
        jnp.transpose(w_widen, (0, 2, 1)),
        w_deep,
        w_upward,
        w_decode,
        w_classes,
        gain_enter,
        shift_enter,
        gain_encode,
        shift_encode,
        gain_widen,
        shift_widen,
        gain_deep,
        shift_deep,
        gain_decode,
        shift_decode,
        bias_classes,
    )
    copies = [pltpu.VMEM(x.shape, x.dtype) for x in operands[:-1]]
    copies.append(pltpu.SMEM((2,), F32))
    logits = pl.pallas_call(
        functools.partial(kernel, n_wide, n_narrow),
        out_shape=jax.ShapeDtypeStruct((64, COLS), F32),
        in_specs=[pl.BlockSpec(memory_space=pltpu.HBM)] * len(operands),
        out_specs=pl.BlockSpec(memory_space=pltpu.VMEM),
        scratch_shapes=copies
        + [
            pltpu.VMEM((32, COLS), F32),
            pltpu.VMEM((32, COLS), BF16),
            pltpu.VMEM((3, 160, COLS), BF16),
            pltpu.VMEM((6, 2, 256, 256), BF16),
            pltpu.VMEM((9, 256, 256), BF16),
            pltpu.VMEM((9, 128, 256), BF16),
            pltpu.VMEM((9, 256, 256), BF16),
            pltpu.VMEM((4, 256, 256), BF16),
            pltpu.VMEM((9, 2, 256, 256), BF16),
            pltpu.VMEM((64, 1024), BF16),
            pltpu.VMEM((6, 256), F32),
            pltpu.VMEM((4, 256), F32),
            pltpu.VMEM((4, 18, XC, 256), BF16),
            pltpu.VMEM((4, 6, XC, 256), BF16),
            pltpu.VMEM((3, 8, XC, 128), BF16),
            pltpu.VMEM((3, 6, XC, 256), BF16),
            pltpu.VMEM((4, 6, XC, 256), BF16),
            pltpu.VMEM((2, ROWS * COLS, 128), F32),
            pltpu.SemaphoreType.DMA((len(operands),)),
            pltpu.SemaphoreType.DMA((len(OFFSETS),)),
            pltpu.SemaphoreType.DMA((len(OFFSETS),)),
        ],
        compiler_params=pltpu.CompilerParams(
            collective_id=0, has_side_effects=True, vmem_limit_bytes=52 * 1024 * 1024
        ),
        name="unet",
    )(*[pltpu.with_memory_space_constraint(x, pltpu.HBM) for x in operands])
    return logits.reshape(2, DEPTH, ROWS, COLS)


def solution(mesh):
    in_specs = (P(None, None, "wide", "narrow"),) + (P(),) * 18
    return jax.shard_map(
        functools.partial(per_device, mesh.shape["wide"], mesh.shape["narrow"]),
        mesh=mesh,
        in_specs=in_specs,
        out_specs=P(None, None, "wide", "narrow"),
        check_vma=False,
    )
```

```python
import functools

import jax
import jax.numpy as jnp
from jax import lax
from jax.experimental import pallas as pl
from jax.experimental.pallas import tpu as pltpu
from jax.sharding import PartitionSpec as P

F32 = jnp.float32
BF16 = jnp.bfloat16
MESH = pl.DeviceIdType.MESH

DEPTH = 8
ROWS = 4
COLS = 128
HALF = 64
XC = 80
OFFSETS = [
    (dy, dx) for dy in (-2, 2, -1, 1, 0) for dx in (-1, 1, 0) if (dy, dx) != (0, 0)
]
SMALL_LOADS = (1,) + tuple(range(7, 19))
LARGE_LOADS = tuple(range(2, 7))
POOL_PLANE = (0, 2, 1, 3)


def iota(shape, dim):
    return lax.broadcasted_iota(jnp.int32, shape, dim)


def dot(a, b):
    return jnp.dot(a, b, preferred_element_type=F32)


def dot_nt(a, b):
    return lax.dot_general(a, b, (((1,), (1,)), ((), ())), preferred_element_type=F32)


def eye(n):
    return (iota((n, n), 0) == iota((n, n), 1)).astype(BF16)


def repeat_matrix(n, total, dtype):
    return (iota((n, total), 0) == (iota((n, total), 1) & (n - 1))).astype(dtype)


def band(lane, width, tile, plane, taps):
    group = lane >> (width.bit_length() - 1)
    first = plane - tile * (128 // width)
    out = jnp.zeros(taps[0].shape, F32)
    for dz in range(3):
        place = first + 1 - dz
        if 0 <= place < 128 // width:
            out = jnp.where(group == place, taps[dz], out)
    return out


def kernel(
    n_wide,
    n_narrow,
    volume,
    w_enter,
    w_encode,
    w_widen,
    w_deep,
    w_upward,
    w_decode,
    w_classes,
    gain_enter,
    shift_enter,
    gain_encode,
    shift_encode,
    gain_widen,
    shift_widen,
    gain_deep,
    shift_deep,
    gain_decode,
    shift_decode,
    bias,
    out,
    v_volume,
    v_enter,
    v_encode,
    v_widen,
    v_deep,
    v_upward,
    v_decode,
    v_classes,
    v_gain_enter,
    v_shift_enter,
    v_gain_encode,
    v_shift_encode,
    v_gain_widen,
    v_shift_widen,
    v_gain_deep,
    v_shift_deep,
    v_gain_decode,
    v_shift_decode,
    s_bias,
    plane_rows,
    own,
    halo,
    m_enter,
    m_encode,
    m_widen,
    m_deep,
    m_upward,
    m_decode,
    m_classes,
    fine,
    coarse,
    first,
    skip,
    pooled,
    widened,
    lifted,
    decoded,
    load_sem,
    send_sem,
    recv_sem,
):
    w = lax.axis_index("wide")
    n = lax.axis_index("narrow")

    def within(at, count):
        return jnp.logical_and(at >= 0, at < count)

    def has(dy, dx):
        return jnp.logical_and(within(w + dy, n_wide), within(n + dx, n_narrow))

    halo[...] = jnp.zeros(halo.shape, BF16)

    barrier = pltpu.get_barrier_semaphore()
    for dy, dx in OFFSETS:

        @pl.when(has(dy, dx))
        def _():
            pl.semaphore_signal(
                barrier, inc=1, device_id=(w + dy, n + dx), device_id_type=MESH
            )

    sources = (
        volume, w_enter, w_encode, w_widen, w_deep, w_upward, w_decode, w_classes,
        gain_enter, shift_enter, gain_encode, shift_encode, gain_widen, shift_widen,
        gain_deep, shift_deep, gain_decode, shift_decode, bias,
    )
    targets = (
        v_volume, v_enter, v_encode, v_widen, v_deep, v_upward, v_decode, v_classes,
        v_gain_enter, v_shift_enter, v_gain_encode, v_shift_encode, v_gain_widen, v_shift_widen,
        v_gain_deep, v_shift_deep, v_gain_decode, v_shift_decode, s_bias,
    )
    loads = [
        pltpu.make_async_copy(source, target, load_sem.at[k])
        for k, (source, target) in enumerate(zip(sources, targets))
    ]
    for load in loads:
        load.start()

    loads[0].wait()
    for z in range(DEPTH):
        plane_rows[ROWS * z : ROWS * (z + 1), :] = v_volume[z].astype(F32)
    by_row = jnp.concatenate(
        [plane_rows[pl.ds(y, DEPTH, stride=ROWS), :] for y in range(ROWS)], axis=0
    )
    by_row = pltpu.roll(by_row, HALF, 1).astype(BF16)
    own[...] = by_row
    halo[1, 64:96, :] = by_row

    for k in SMALL_LOADS:
        loads[k].wait()

    def rows_of(refs):
        return jnp.concatenate([ref[...].reshape(1, ref.shape[0]) for ref in refs], axis=0)

    fine[...] = jnp.dot(
        rows_of((v_gain_enter, v_shift_enter, v_gain_encode, v_shift_encode, v_gain_decode, v_shift_decode)),
        repeat_matrix(32, 256, F32),
        preferred_element_type=F32,
        precision=lax.Precision.HIGHEST,
    )
    coarse[...] = jnp.dot(
        rows_of((v_gain_widen, v_shift_widen, v_gain_deep, v_shift_deep)),
        repeat_matrix(64, 256, F32),
        preferred_element_type=F32,
        precision=lax.Precision.HIGHEST,
    )

    taps = dot(v_enter[...], repeat_matrix(32, 256, BF16))
    offset_of = iota((DEPTH, 256), 0) - (iota((DEPTH, 256), 1) >> 5) + 1
    zero = jnp.zeros((DEPTH, 256), F32)
    blocks = {}
    for dx in range(3):
        for dy in range(3):
            block = zero
            for dz in range(3):
                row = 9 * dz + 3 * dy + dx
                block = jnp.where(
                    offset_of == dz, jnp.broadcast_to(taps[row : row + 1], (DEPTH, 256)), block
                )
            blocks[dx, dy] = block
    for yo in range(5):
        for px in range(2):
            pieces = [
                blocks.get((s - px, yin - yo), zero) for s in range(4) for yin in range(8)
            ]
            m_enter[yo, px] = jnp.concatenate(pieces, axis=0).astype(BF16)

    classes = dot(v_classes[...], repeat_matrix(32, 256, BF16))
    at_row = iota((64, 256), 0)
    at_lane = iota((64, 256), 1)
    per_class = jnp.where(
        at_row < 32,
        jnp.broadcast_to(classes[0:1], (64, 256)),
        jnp.broadcast_to(classes[1:2], (64, 256)),
    )
    per_plane = jnp.where(((at_row & 31) >> 2) == (at_lane >> 5), per_class, 0.0)
    for y in range(ROWS):
        m_classes[:, 256 * y : 256 * (y + 1)] = jnp.where(
            (at_row & 3) == y, per_plane, 0.0
        ).astype(BF16)

    def exchange(k):
        dy, dx = OFFSETS[k]
        return pltpu.make_async_remote_copy(
            src_ref=own,
            dst_ref=halo.at[1 - dx, pl.ds(32 * (2 - dy), 32)],
            send_sem=send_sem.at[k],
            recv_sem=recv_sem.at[k],
            device_id=(w + dy, n + dx),
            device_id_type=MESH,
        )

    pl.semaphore_wait(barrier, sum(has(dy, dx).astype(jnp.int32) for dy, dx in OFFSETS))
    for k, (dy, dx) in enumerate(OFFSETS):

        @pl.when(has(dy, dx))
        def _():
            exchange(k).start()

    for k in LARGE_LOADS:
        loads[k].wait()

    eye32 = eye(32)
    eye64 = eye(64)
    repeat64 = repeat_matrix(64, 128, BF16)
    lane32 = iota((32, 128), 1)
    lane64 = iota((64, 128), 1)

    def build_fine(dy, carry):
        for dx in range(3):
            tap = 3 * dy + dx
            rows = [v_encode[9 * dz + tap] for dz in range(3) for _ in range(4)]
            turned = dot_nt(eye32, jnp.concatenate(rows, axis=0))
            parts = [turned[:, 128 * dz : 128 * (dz + 1)] for dz in range(3)]
            for z in range(DEPTH):
                for tile in range(2):
                    m_encode[tap, 32 * z : 32 * (z + 1), 128 * tile : 128 * (tile + 1)] = band(
                        lane32, 32, tile, z, parts
                    ).astype(BF16)
            rows = [v_decode[9 * dz + tap] for dz in range(3) for _ in range(4)]
            turned = dot_nt(eye64, jnp.concatenate(rows, axis=0))
            for source in range(2):
                parts = [
                    turned[32 * source : 32 * (source + 1), 128 * dz : 128 * (dz + 1)]
                    for dz in range(3)
                ]
                for z in range(DEPTH):
                    for tile in range(2):
                        m_decode[
                            source, tap, 32 * z : 32 * (z + 1), 128 * tile : 128 * (tile + 1)
                        ] = band(lane32, 32, tile, z, parts).astype(BF16)
        return carry

    lax.fori_loop(0, 3, build_fine, 0)

    def build_coarse(dy, carry):
        for dx in range(3):
            tap = 3 * dy + dx
            rows = [v_widen[9 * dz + tap] for dz in range(3)]
            turned = dot(jnp.concatenate(rows, axis=0), repeat64)
            parts = [turned[32 * dz : 32 * (dz + 1)] for dz in range(3)]
            for group in range(4):
                for tile in range(2):
                    m_widen[
                        tap, 32 * group : 32 * (group + 1), 128 * tile : 128 * (tile + 1)
                    ] = band(lane32, 64, tile, POOL_PLANE[group], parts).astype(BF16)
            rows = [v_deep[9 * dz + tap] for dz in range(3) for _ in range(2)]
            turned = dot_nt(eye64, jnp.concatenate(rows, axis=0))
            parts = [turned[:, 128 * dz : 128 * (dz + 1)] for dz in range(3)]
            for z in range(4):
                for tile in range(2):
                    m_deep[tap, 64 * z : 64 * (z + 1), 128 * tile : 128 * (tile + 1)] = band(
                        lane64, 64, tile, z, parts
                    ).astype(BF16)
        return carry

    lax.fori_loop(0, 3, build_coarse, 0)

    for tap in range(4):
        rows = [v_upward[4 * a + tap] for _ in range(2) for a in range(2)]
        turned = dot_nt(eye64, jnp.concatenate(rows, axis=0))
        for z in range(4):
            for tile in range(2):
                m_upward[tap, 64 * z : 64 * (z + 1), 128 * tile : 128 * (tile + 1)] = jnp.where(
                    (lane64 >> 6) == z - 2 * tile, turned, 0.0
                ).astype(BF16)

    def inside(at, count):
        return within(at, count).astype(F32)

    left = inside(n - 1, n_narrow)
    right = inside(n + 1, n_narrow)

    def relu_inside(acc, gain, shift, keep):
        gain = gain * keep
        shift = shift * keep
        return jnp.concatenate(
            [
                jnp.maximum(acc[0:64] * gain + shift, 0.0),
                jnp.maximum(acc[64:72] * (gain * right) + shift * right, 0.0),
                jnp.maximum(acc[72:80] * (gain * left) + shift * left, 0.0),
            ],
            axis=0,
        )

    def put_columns(ref, row, parity, value):
        ref[(1 + parity, *row)] = value.astype(BF16)
        if parity == 0:
            ref[(3, *row)] = pltpu.roll(value, XC - 1, 0).astype(BF16)
        else:
            ref[(0, *row)] = pltpu.roll(value, 1, 0).astype(BF16)

    lane = iota((96, 128), 1)
    at = iota((XC, 256), 0)
    pick = (
        iota((XC, 256), 1) == 2 * jnp.where(at < 72, at, at - XC) + HALF
    ).astype(BF16)
    pool_lane = (iota((XC, 128), 1) & 32) == 0
    encode_matrix = m_encode[...].reshape(9 * 256, 256)
    near = jnp.where(lax.rem(w, 4) < 2, 1, 0)

    for turn in range(2):
        half = near if turn == 0 else 1 - near
        for k, (dy, dx) in enumerate(OFFSETS):
            first_half = 1 if dy < 0 else 0
            if dy == 0:
                now = turn == 0
            else:
                now = near == first_half if turn == 0 else near != first_half

            @pl.when(jnp.logical_and(has(-dy, -dx), now))
            def _():
                exchange(k).wait_recv()

        rows = pl.ds(pl.multiple_of(64 * half, 64), 96)
        before, middle, after = [halo[side, rows, :].astype(F32) for side in range(3)]
        wide_rows = jnp.concatenate(
            [jnp.where(lane < HALF, before, middle), jnp.where(lane < HALF, middle, after)],
            axis=1,
        )
        wide_rows = jnp.concatenate([wide_rows, jnp.zeros((8, 256), F32)], axis=0)
        shifted = [
            wide_rows if s == 1 else pltpu.roll(wide_rows, (1 - s) % 256, 1) for s in range(4)
        ]
        columns = jnp.concatenate(
            [
                dot_nt(
                    pick,
                    jnp.concatenate(
                        [piece[40 * g : 40 * g + 64] for piece in shifted], axis=0
                    ).astype(BF16),
                ).astype(BF16)
                for g in range(2)
            ],
            axis=0,
        )

        for yo in range(5):
            for px in range(2):
                acc = dot(columns, m_enter[yo, px])
                for g in range(2):
                    row = 5 * g + yo
                    keep = inside(w * ROWS - 7 + 8 * half + row, n_wide * ROWS)
                    put_columns(
                        first, (turn, row), px,
                        relu_inside(
                            acc[XC * g : XC * (g + 1)], fine[0:1, :], fine[1:2, :], keep
                        ),
                    )

        parity_acc = []
        for px in range(2):
            pieces = [
                first[px + dx, turn, dy : dy + 8].reshape(8 * XC, 256)
                for dy in range(3)
                for dx in range(3)
            ]
            parity_acc.append(dot(jnp.concatenate(pieces, axis=1), encode_matrix))
        for k in range(4):
            keep = inside(w * 2 - 3 + 4 * half + k, n_wide * 2)
            best = None
            for y in range(2):
                row = 2 * k + y
                for px in range(2):
                    value = relu_inside(
                        parity_acc[px][XC * row : XC * (row + 1)],
                        fine[2:3, :], fine[3:4, :], keep,
                    )
                    if row not in (3, 4):
                        put_columns(skip, (8 * half + row,), px, value)
                    best = value if best is None else jnp.maximum(best, value)
            low = best[:, 0:128]
            high = best[:, 128:256]
            low = jnp.maximum(low, pltpu.roll(low, 96, 1))
            high = jnp.maximum(high, pltpu.roll(high, 96, 1))
            best = jnp.where(pool_lane, low, pltpu.roll(high, 32, 1))
            pooled[0, 4 * half + k] = pltpu.roll(best, 1, 0).astype(BF16)
            pooled[1, 4 * half + k] = best.astype(BF16)
            pooled[2, 4 * half + k] = pltpu.roll(best, XC - 1, 0).astype(BF16)

    def decode_part(px, source):
        ref, start = ((skip, 5), (lifted, 0))[source]
        pieces = [
            ref[px + dx, start + dy : start + dy + ROWS, 0:HALF].reshape(ROWS * HALF, 256)
            for dy in range(3)
            for dx in range(3)
        ]
        return dot(
            jnp.concatenate(pieces, axis=1), m_decode[source].reshape(9 * 256, 256)
        )

    from_skip = [decode_part(0, 0)]

    pieces = [
        pooled[dx, dy : dy + 6].reshape(6 * XC, 128) for dy in range(3) for dx in range(3)
    ]
    acc = dot(jnp.concatenate(pieces, axis=1), m_widen[...].reshape(9 * 128, 256))
    from_skip.append(decode_part(1, 0))
    for k in range(6):
        keep = inside(w * 2 - 2 + k, n_wide * 2)
        value = relu_inside(acc[XC * k : XC * (k + 1)], coarse[0:1, :], coarse[1:2, :], keep)
        widened[0, k] = pltpu.roll(value, 1, 0).astype(BF16)
        widened[1, k] = value.astype(BF16)
        widened[2, k] = pltpu.roll(value, XC - 1, 0).astype(BF16)

    pieces = [
        widened[dx, dy : dy + 4].reshape(4 * XC, 256) for dy in range(3) for dx in range(3)
    ]
    acc = dot(jnp.concatenate(pieces, axis=1), m_deep[...].reshape(9 * 256, 256))
    deepest = jnp.concatenate(
        [
            relu_inside(
                acc[XC * k : XC * (k + 1)],
                coarse[2:3, :],
                coarse[3:4, :],
                inside(w * 2 - 1 + k, n_wide * 2),
            )
            for k in range(4)
        ],
        axis=0,
    ).astype(BF16)

    for b in range(2):
        source = deepest[XC * (1 - b) : XC * (4 - b)]
        for e in range(2):
            acc = dot(source, m_upward[2 * b + e])
            for k in range(3):
                put_columns(lifted, (2 * k + 1 - b,), e, acc[XC * k : XC * (k + 1)])

    acc = jnp.concatenate([from_skip[px] + decode_part(px, 1) for px in range(2)], axis=0)
    value = jnp.maximum(acc * fine[4:5, :] + fine[5:6, :], 0.0)
    for px in range(2):
        for y in range(ROWS):
            start = (px * ROWS + y) * HALF
            for tile in range(2):
                decoded[tile, pl.ds(y * COLS + px, HALF, stride=2), :] = value[
                    start : start + HALF, 128 * tile : 128 * (tile + 1)
                ]

    features = jnp.concatenate(
        [
            decoded[tile, y * COLS : (y + 1) * COLS, :].astype(BF16)
            for y in range(ROWS)
            for tile in range(2)
        ],
        axis=1,
    )
    logits = dot_nt(m_classes[...], features)
    for k, (dy, dx) in enumerate(OFFSETS):

        @pl.when(has(dy, dx))
        def _():
            exchange(k).wait_send()

    out[...] = logits + jnp.where(iota((64, 128), 0) < 32, s_bias[0], s_bias[1])


def per_device(
    n_wide,
    n_narrow,
    volume,
    w_enter,
    gain_enter,
    shift_enter,
    w_encode,
    gain_encode,
    shift_encode,
    w_widen,
    gain_widen,
    shift_widen,
    w_deep,
    gain_deep,
    shift_deep,
    w_upward,
    w_decode,
    gain_decode,
    shift_decode,
    w_classes,
    bias_classes,
):
    operands = (
        volume.reshape(DEPTH, ROWS, COLS),
        w_enter.reshape(27, 32),
        w_encode,
        jnp.transpose(w_widen, (0, 2, 1)),
        w_deep,
        w_upward,
        w_decode,
        w_classes,
        gain_enter,
        shift_enter,
        gain_encode,
        shift_encode,
        gain_widen,
        shift_widen,
        gain_deep,
        shift_deep,
        gain_decode,
        shift_decode,
        bias_classes,
    )
    copies = [pltpu.VMEM(x.shape, x.dtype) for x in operands[:-1]]
    copies.append(pltpu.SMEM((2,), F32))
    logits = pl.pallas_call(
        functools.partial(kernel, n_wide, n_narrow),
        out_shape=jax.ShapeDtypeStruct((64, COLS), F32),
        in_specs=[pl.BlockSpec(memory_space=pltpu.HBM)] * len(operands),
        out_specs=pl.BlockSpec(memory_space=pltpu.VMEM),
        scratch_shapes=copies
        + [
            pltpu.VMEM((32, COLS), F32),
            pltpu.VMEM((32, COLS), BF16),
            pltpu.VMEM((3, 160, COLS), BF16),
            pltpu.VMEM((5, 2, 256, 256), BF16),
            pltpu.VMEM((9, 256, 256), BF16),
            pltpu.VMEM((9, 128, 256), BF16),
            pltpu.VMEM((9, 256, 256), BF16),
            pltpu.VMEM((4, 256, 256), BF16),
            pltpu.VMEM((2, 9, 256, 256), BF16),
            pltpu.VMEM((64, 1024), BF16),
            pltpu.VMEM((6, 256), F32),
            pltpu.VMEM((4, 256), F32),
            pltpu.VMEM((4, 2, 10, XC, 256), BF16),
            pltpu.VMEM((4, 16, XC, 256), BF16),
            pltpu.VMEM((3, 8, XC, 128), BF16),
            pltpu.VMEM((3, 6, XC, 256), BF16),
            pltpu.VMEM((4, 6, XC, 256), BF16),
            pltpu.VMEM((2, ROWS * COLS, 128), F32),
            pltpu.SemaphoreType.DMA((len(operands),)),
            pltpu.SemaphoreType.DMA((len(OFFSETS),)),
            pltpu.SemaphoreType.DMA((len(OFFSETS),)),
        ],
        compiler_params=pltpu.CompilerParams(
            collective_id=0, has_side_effects=True, vmem_limit_bytes=52 * 1024 * 1024
        ),
        name="unet",
    )(*[pltpu.with_memory_space_constraint(x, pltpu.HBM) for x in operands])
    return logits.reshape(2, DEPTH, ROWS, COLS)


def solution(mesh):
    in_specs = (P(None, None, "wide", "narrow"),) + (P(),) * 18
    return jax.shard_map(
        functools.partial(per_device, mesh.shape["wide"], mesh.shape["narrow"]),
        mesh=mesh,
        in_specs=in_specs,
        out_specs=P(None, None, "wide", "narrow"),
        check_vma=False,
    )
```

```python
import functools

import jax
import jax.numpy as jnp
from jax import lax
from jax.experimental import pallas as pl
from jax.experimental.pallas import tpu as pltpu
from jax.sharding import PartitionSpec as P

F32 = jnp.float32
BF16 = jnp.bfloat16
MESH = pl.DeviceIdType.MESH

DEPTH = 8
ROWS = 4
COLS = 128
HALF = 64
XC = 80
OFFSETS = [
    (dy, dx) for dy in (-2, 2, -1, 1, 0) for dx in (-1, 1, 0) if (dy, dx) != (0, 0)
]
SMALL_LOADS = (1,) + tuple(range(7, 19))
LARGE_LOADS = tuple(range(2, 7))
POOL_PLANE = (0, 2, 1, 3)


def iota(shape, dim):
    return lax.broadcasted_iota(jnp.int32, shape, dim)


def dot(a, b):
    return jnp.dot(a, b, preferred_element_type=F32)


def dot_nt(a, b):
    return lax.dot_general(a, b, (((1,), (1,)), ((), ())), preferred_element_type=F32)


def eye(n):
    return (iota((n, n), 0) == iota((n, n), 1)).astype(BF16)


def repeat_matrix(n, total, dtype):
    return (iota((n, total), 0) == (iota((n, total), 1) & (n - 1))).astype(dtype)


def bands(width, taps):
    count = 128 // width
    lane = iota(taps[0].shape, 1)
    places = [((lane >> (width.bit_length() - 1)) == p).astype(BF16) for p in range(count)]
    placed = [[tap.astype(BF16) * place for place in places] for tap in taps]
    blocks = {}
    for first in range(-1, count + 1):
        terms = [
            placed[dz][first + 1 - dz] for dz in range(3) if 0 <= first + 1 - dz < count
        ]
        blocks[first] = functools.reduce(jnp.add, terms)
    return blocks


def kernel(
    n_wide,
    n_narrow,
    volume,
    w_enter,
    w_encode,
    w_widen,
    w_deep,
    w_upward,
    w_decode,
    w_classes,
    gain_enter,
    shift_enter,
    gain_encode,
    shift_encode,
    gain_widen,
    shift_widen,
    gain_deep,
    shift_deep,
    gain_decode,
    shift_decode,
    bias,
    out,
    v_volume,
    v_enter,
    v_encode,
    v_widen,
    v_deep,
    v_upward,
    v_decode,
    v_classes,
    v_gain_enter,
    v_shift_enter,
    v_gain_encode,
    v_shift_encode,
    v_gain_widen,
    v_shift_widen,
    v_gain_deep,
    v_shift_deep,
    v_gain_decode,
    v_shift_decode,
    s_bias,
    plane_rows,
    own,
    halo,
    m_enter,
    m_encode,
    m_widen,
    m_deep,
    m_upward,
    m_decode,
    m_classes,
    fine,
    coarse,
    first,
    skip,
    pooled,
    widened,
    lifted,
    decoded,
    load_sem,
    send_sem,
    recv_sem,
):
    w = lax.axis_index("wide")
    n = lax.axis_index("narrow")

    def within(at, count):
        return jnp.logical_and(at >= 0, at < count)

    def has(dy, dx):
        return jnp.logical_and(within(w + dy, n_wide), within(n + dx, n_narrow))

    halo[...] = jnp.zeros(halo.shape, BF16)

    barrier = pltpu.get_barrier_semaphore()
    for dy, dx in OFFSETS:

        @pl.when(has(dy, dx))
        def _():
            pl.semaphore_signal(
                barrier, inc=1, device_id=(w + dy, n + dx), device_id_type=MESH
            )

    sources = (
        volume, w_enter, w_encode, w_widen, w_deep, w_upward, w_decode, w_classes,
        gain_enter, shift_enter, gain_encode, shift_encode, gain_widen, shift_widen,
        gain_deep, shift_deep, gain_decode, shift_decode, bias,
    )
    targets = (
        v_volume, v_enter, v_encode, v_widen, v_deep, v_upward, v_decode, v_classes,
        v_gain_enter, v_shift_enter, v_gain_encode, v_shift_encode, v_gain_widen, v_shift_widen,
        v_gain_deep, v_shift_deep, v_gain_decode, v_shift_decode, s_bias,
    )
    loads = [
        pltpu.make_async_copy(source, target, load_sem.at[k])
        for k, (source, target) in enumerate(zip(sources, targets))
    ]
    for load in loads:
        load.start()

    loads[0].wait()
    for z in range(DEPTH):
        plane_rows[ROWS * z : ROWS * (z + 1), :] = v_volume[z].astype(F32)
    by_row = jnp.concatenate(
        [plane_rows[pl.ds(y, DEPTH, stride=ROWS), :] for y in range(ROWS)], axis=0
    )
    by_row = pltpu.roll(by_row, HALF, 1).astype(BF16)
    own[...] = by_row
    halo[1, 64:96, :] = by_row

    def exchange(k):
        dy, dx = OFFSETS[k]
        return pltpu.make_async_remote_copy(
            src_ref=own,
            dst_ref=halo.at[1 - dx, pl.ds(32 * (2 - dy), 32)],
            send_sem=send_sem.at[k],
            recv_sem=recv_sem.at[k],
            device_id=(w + dy, n + dx),
            device_id_type=MESH,
        )

    pl.semaphore_wait(barrier, sum(has(dy, dx).astype(jnp.int32) for dy, dx in OFFSETS))
    for k, (dy, dx) in enumerate(OFFSETS):

        @pl.when(has(dy, dx))
        def _():
            exchange(k).start()

    for k in SMALL_LOADS:
        loads[k].wait()

    def rows_of(refs):
        return jnp.concatenate([ref[...].reshape(1, ref.shape[0]) for ref in refs], axis=0)

    fine[...] = jnp.dot(
        rows_of((v_gain_enter, v_shift_enter, v_gain_encode, v_shift_encode, v_gain_decode, v_shift_decode)),
        repeat_matrix(32, 256, F32),
        preferred_element_type=F32,
        precision=lax.Precision.HIGHEST,
    )
    coarse[...] = jnp.dot(
        rows_of((v_gain_widen, v_shift_widen, v_gain_deep, v_shift_deep)),
        repeat_matrix(64, 256, F32),
        preferred_element_type=F32,
        precision=lax.Precision.HIGHEST,
    )

    taps = dot(v_enter[...], repeat_matrix(32, 256, BF16))
    offset_of = iota((DEPTH, 256), 0) - (iota((DEPTH, 256), 1) >> 5) + 1
    zero = jnp.zeros((DEPTH, 256), F32)
    blocks = {}
    for dx in range(3):
        for dy in range(3):
            block = zero
            for dz in range(3):
                row = 9 * dz + 3 * dy + dx
                block = jnp.where(
                    offset_of == dz, jnp.broadcast_to(taps[row : row + 1], (DEPTH, 256)), block
                )
            blocks[dx, dy] = block
    for yo in range(5):
        for px in range(2):
            pieces = [
                blocks.get((s - px, yin - yo), zero) for s in range(4) for yin in range(8)
            ]
            m_enter[yo, px] = jnp.concatenate(pieces, axis=0).astype(BF16)

    classes = dot(v_classes[...], repeat_matrix(32, 256, BF16))
    at_row = iota((64, 256), 0)
    at_lane = iota((64, 256), 1)
    per_class = jnp.where(
        at_row < 32,
        jnp.broadcast_to(classes[0:1], (64, 256)),
        jnp.broadcast_to(classes[1:2], (64, 256)),
    )
    per_plane = jnp.where(((at_row & 31) >> 2) == (at_lane >> 5), per_class, 0.0)
    for y in range(ROWS):
        m_classes[:, 256 * y : 256 * (y + 1)] = jnp.where(
            (at_row & 3) == y, per_plane, 0.0
        ).astype(BF16)

    for k in LARGE_LOADS:
        loads[k].wait()

    repeat64 = repeat_matrix(64, 128, BF16)
    lane64 = iota((64, 128), 1)
    zero32 = jnp.zeros((32, 128), BF16)
    zero64 = jnp.zeros((64, 128), BF16)

    eye256 = eye(256)

    def turn_taps(ref):
        channels = ref.shape[2]
        count = 256 // channels
        turned = []
        for start in range(0, 27, count):
            row = jnp.concatenate(
                [ref[min(start + k, 26)] for k in range(count)], axis=1
            )
            result = dot_nt(
                eye256, jnp.concatenate([row] * (128 // ref.shape[1]), axis=0)
            ).astype(BF16)
            turned += [result[channels * k : channels * (k + 1)] for k in range(count)]
        return turned

    from_encode = turn_taps(v_encode)
    from_decode = turn_taps(v_decode)
    for tap in range(9):
        blocks = bands(32, [from_encode[9 * dz + tap] for dz in range(3)])
        for z in range(DEPTH):
            for tile in range(2):
                m_encode[tap, 32 * z : 32 * (z + 1), 128 * tile : 128 * (tile + 1)] = (
                    blocks.get(z - 4 * tile, zero32)
                )
        for source in range(2):
            blocks = bands(
                32,
                [from_decode[9 * dz + tap][32 * source : 32 * (source + 1)] for dz in range(3)],
            )
            for z in range(DEPTH):
                for tile in range(2):
                    m_decode[
                        source, tap, 32 * z : 32 * (z + 1), 128 * tile : 128 * (tile + 1)
                    ] = blocks.get(z - 4 * tile, zero32)

    from_widen = dot(v_widen[...].reshape(27 * 32, 64), repeat64).astype(BF16)
    from_deep = turn_taps(v_deep)
    for tap in range(9):
        starts = [32 * (9 * dz + tap) for dz in range(3)]
        blocks = bands(64, [from_widen[start : start + 32] for start in starts])
        for group in range(4):
            for tile in range(2):
                m_widen[
                    tap, 32 * group : 32 * (group + 1), 128 * tile : 128 * (tile + 1)
                ] = blocks.get(POOL_PLANE[group] - 2 * tile, zero32)
        blocks = bands(64, [from_deep[9 * dz + tap] for dz in range(3)])
        for z in range(4):
            for tile in range(2):
                m_deep[tap, 64 * z : 64 * (z + 1), 128 * tile : 128 * (tile + 1)] = (
                    blocks.get(z - 2 * tile, zero64)
                )

    rows = [
        jnp.concatenate([v_upward[4 * a + tap] for tap in range(4)], axis=1) for a in range(2)
    ]
    turned = dot_nt(eye256, jnp.concatenate(rows + rows, axis=0)).astype(BF16)
    halves = [((lane64 >> 6) == half).astype(BF16) for half in range(2)]
    for tap in range(4):
        block = turned[64 * tap : 64 * (tap + 1)]
        for z in range(4):
            for tile in range(2):
                m_upward[tap, 64 * z : 64 * (z + 1), 128 * tile : 128 * (tile + 1)] = (
                    block * halves[z - 2 * tile] if 0 <= z - 2 * tile < 2 else zero64
                )

    def inside(at, count):
        return within(at, count).astype(F32)

    left = inside(n - 1, n_narrow)
    right = inside(n + 1, n_narrow)

    def relu_inside(acc, gain, shift, keep):
        gain = gain * keep
        shift = shift * keep
        return jnp.concatenate(
            [
                jnp.maximum(acc[0:64] * gain + shift, 0.0),
                jnp.maximum(acc[64:72] * (gain * right) + shift * right, 0.0),
                jnp.maximum(acc[72:80] * (gain * left) + shift * left, 0.0),
            ],
            axis=0,
        )

    def put_columns(ref, row, parity, value):
        ref[(1 + parity, *row)] = value.astype(BF16)
        if parity == 0:
            ref[(3, *row)] = pltpu.roll(value, XC - 1, 0).astype(BF16)
        else:
            ref[(0, *row)] = pltpu.roll(value, 1, 0).astype(BF16)

    lane = iota((96, 128), 1)
    at = iota((XC, 256), 0)
    pick = (
        iota((XC, 256), 1) == 2 * jnp.where(at < 72, at, at - XC) + HALF
    ).astype(BF16)
    pool_lane = (iota((XC, 128), 1) & 32) == 0
    encode_matrix = m_encode[...].reshape(9 * 256, 256)
    near = jnp.where(lax.rem(w, 4) < 2, 1, 0)

    for turn in range(2):
        half = near if turn == 0 else 1 - near
        for k, (dy, dx) in enumerate(OFFSETS):
            first_half = 1 if dy < 0 else 0
            if dy == 0:
                now = turn == 0
            else:
                now = near == first_half if turn == 0 else near != first_half

            @pl.when(jnp.logical_and(has(-dy, -dx), now))
            def _():
                exchange(k).wait_recv()

        rows = pl.ds(pl.multiple_of(64 * half, 64), 96)
        before, middle, after = [halo[side, rows, :].astype(F32) for side in range(3)]
        wide_rows = jnp.concatenate(
            [jnp.where(lane < HALF, before, middle), jnp.where(lane < HALF, middle, after)],
            axis=1,
        )
        wide_rows = jnp.concatenate([wide_rows, jnp.zeros((8, 256), F32)], axis=0)
        shifted = [
            wide_rows if s == 1 else pltpu.roll(wide_rows, (1 - s) % 256, 1) for s in range(4)
        ]
        columns = jnp.concatenate(
            [
                dot_nt(
                    pick,
                    jnp.concatenate(
                        [piece[40 * g : 40 * g + 64] for piece in shifted], axis=0
                    ).astype(BF16),
                ).astype(BF16)
                for g in range(2)
            ],
            axis=0,
        )

        for yo in range(5):
            for px in range(2):
                acc = dot(columns, m_enter[yo, px])
                for g in range(2):
                    row = 5 * g + yo
                    keep = inside(w * ROWS - 7 + 8 * half + row, n_wide * ROWS)
                    put_columns(
                        first, (turn, row), px,
                        relu_inside(
                            acc[XC * g : XC * (g + 1)], fine[0:1, :], fine[1:2, :], keep
                        ),
                    )

        parity_acc = []
        for px in range(2):
            pieces = [
                first[px + dx, turn, dy : dy + 8].reshape(8 * XC, 256)
                for dy in range(3)
                for dx in range(3)
            ]
            parity_acc.append(dot(jnp.concatenate(pieces, axis=1), encode_matrix))
        for k in range(4):
            keep = inside(w * 2 - 3 + 4 * half + k, n_wide * 2)
            best = None
            for y in range(2):
                row = 2 * k + y
                for px in range(2):
                    value = relu_inside(
                        parity_acc[px][XC * row : XC * (row + 1)],
                        fine[2:3, :], fine[3:4, :], keep,
                    )
                    if row not in (3, 4):
                        put_columns(skip, (8 * half + row,), px, value)
                    best = value if best is None else jnp.maximum(best, value)
            low = best[:, 0:128]
            high = best[:, 128:256]
            low = jnp.maximum(low, pltpu.roll(low, 96, 1))
            high = jnp.maximum(high, pltpu.roll(high, 96, 1))
            best = jnp.where(pool_lane, low, pltpu.roll(high, 32, 1))
            pooled[0, 4 * half + k] = pltpu.roll(best, 1, 0).astype(BF16)
            pooled[1, 4 * half + k] = best.astype(BF16)
            pooled[2, 4 * half + k] = pltpu.roll(best, XC - 1, 0).astype(BF16)

    def decode_part(px, source):
        ref, start = ((skip, 5), (lifted, 0))[source]
        pieces = [
            ref[px + dx, start + dy : start + dy + ROWS, 0:HALF].reshape(ROWS * HALF, 256)
            for dy in range(3)
            for dx in range(3)
        ]
        return dot(
            jnp.concatenate(pieces, axis=1), m_decode[source].reshape(9 * 256, 256)
        )

    from_skip = [decode_part(0, 0)]

    pieces = [
        pooled[dx, dy : dy + 6].reshape(6 * XC, 128) for dy in range(3) for dx in range(3)
    ]
    acc = dot(jnp.concatenate(pieces, axis=1), m_widen[...].reshape(9 * 128, 256))
    from_skip.append(decode_part(1, 0))
    for k in range(6):
        keep = inside(w * 2 - 2 + k, n_wide * 2)
        value = relu_inside(acc[XC * k : XC * (k + 1)], coarse[0:1, :], coarse[1:2, :], keep)
        widened[0, k] = pltpu.roll(value, 1, 0).astype(BF16)
        widened[1, k] = value.astype(BF16)
        widened[2, k] = pltpu.roll(value, XC - 1, 0).astype(BF16)

    pieces = [
        widened[dx, dy : dy + 4].reshape(4 * XC, 256) for dy in range(3) for dx in range(3)
    ]
    acc = dot(jnp.concatenate(pieces, axis=1), m_deep[...].reshape(9 * 256, 256))
    deepest = jnp.concatenate(
        [
            relu_inside(
                acc[XC * k : XC * (k + 1)],
                coarse[2:3, :],
                coarse[3:4, :],
                inside(w * 2 - 1 + k, n_wide * 2),
            )
            for k in range(4)
        ],
        axis=0,
    ).astype(BF16)

    for b in range(2):
        source = deepest[XC * (1 - b) : XC * (4 - b)]
        for e in range(2):
            acc = dot(source, m_upward[2 * b + e])
            for k in range(3):
                put_columns(lifted, (2 * k + 1 - b,), e, acc[XC * k : XC * (k + 1)])

    acc = jnp.concatenate([from_skip[px] + decode_part(px, 1) for px in range(2)], axis=0)
    value = jnp.maximum(acc * fine[4:5, :] + fine[5:6, :], 0.0)
    for px in range(2):
        for y in range(ROWS):
            start = (px * ROWS + y) * HALF
            for tile in range(2):
                decoded[tile, pl.ds(y * COLS + px, HALF, stride=2), :] = value[
                    start : start + HALF, 128 * tile : 128 * (tile + 1)
                ]

    features = jnp.concatenate(
        [
            decoded[tile, y * COLS : (y + 1) * COLS, :].astype(BF16)
            for y in range(ROWS)
            for tile in range(2)
        ],
        axis=1,
    )
    logits = dot_nt(m_classes[...], features)
    for k, (dy, dx) in enumerate(OFFSETS):

        @pl.when(has(dy, dx))
        def _():
            exchange(k).wait_send()

    out[...] = logits + jnp.where(iota((64, 128), 0) < 32, s_bias[0], s_bias[1])


def per_device(
    n_wide,
    n_narrow,
    volume,
    w_enter,
    gain_enter,
    shift_enter,
    w_encode,
    gain_encode,
    shift_encode,
    w_widen,
    gain_widen,
    shift_widen,
    w_deep,
    gain_deep,
    shift_deep,
    w_upward,
    w_decode,
    gain_decode,
    shift_decode,
    w_classes,
    bias_classes,
):
    operands = (
        volume.reshape(DEPTH, ROWS, COLS),
        w_enter.reshape(27, 32),
        w_encode,
        jnp.transpose(w_widen, (0, 2, 1)),
        w_deep,
        w_upward,
        w_decode,
        w_classes,
        gain_enter,
        shift_enter,
        gain_encode,
        shift_encode,
        gain_widen,
        shift_widen,
        gain_deep,
        shift_deep,
        gain_decode,
        shift_decode,
        bias_classes,
    )
    copies = [pltpu.VMEM(x.shape, x.dtype) for x in operands[:-1]]
    copies.append(pltpu.SMEM((2,), F32))
    logits = pl.pallas_call(
        functools.partial(kernel, n_wide, n_narrow),
        out_shape=jax.ShapeDtypeStruct((64, COLS), F32),
        in_specs=[pl.BlockSpec(memory_space=pltpu.HBM)] * len(operands),
        out_specs=pl.BlockSpec(memory_space=pltpu.VMEM),
        scratch_shapes=copies
        + [
            pltpu.VMEM((32, COLS), F32),
            pltpu.VMEM((32, COLS), BF16),
            pltpu.VMEM((3, 160, COLS), BF16),
            pltpu.VMEM((5, 2, 256, 256), BF16),
            pltpu.VMEM((9, 256, 256), BF16),
            pltpu.VMEM((9, 128, 256), BF16),
            pltpu.VMEM((9, 256, 256), BF16),
            pltpu.VMEM((4, 256, 256), BF16),
            pltpu.VMEM((2, 9, 256, 256), BF16),
            pltpu.VMEM((64, 1024), BF16),
            pltpu.VMEM((6, 256), F32),
            pltpu.VMEM((4, 256), F32),
            pltpu.VMEM((4, 2, 10, XC, 256), BF16),
            pltpu.VMEM((4, 16, XC, 256), BF16),
            pltpu.VMEM((3, 8, XC, 128), BF16),
            pltpu.VMEM((3, 6, XC, 256), BF16),
            pltpu.VMEM((4, 6, XC, 256), BF16),
            pltpu.VMEM((2, ROWS * COLS, 128), F32),
            pltpu.SemaphoreType.DMA((len(operands),)),
            pltpu.SemaphoreType.DMA((len(OFFSETS),)),
            pltpu.SemaphoreType.DMA((len(OFFSETS),)),
        ],
        compiler_params=pltpu.CompilerParams(
            collective_id=0, has_side_effects=True, vmem_limit_bytes=52 * 1024 * 1024
        ),
        name="unet",
    )(*[pltpu.with_memory_space_constraint(x, pltpu.HBM) for x in operands])
    return logits.reshape(2, DEPTH, ROWS, COLS)


def solution(mesh):
    in_specs = (P(None, None, "wide", "narrow"),) + (P(),) * 18
    return jax.shard_map(
        functools.partial(per_device, mesh.shape["wide"], mesh.shape["narrow"]),
        mesh=mesh,
        in_specs=in_specs,
        out_specs=P(None, None, "wide", "narrow"),
        check_vma=False,
    )
```

```python
import functools

import jax
import jax.numpy as jnp
from jax import lax
from jax.experimental import pallas as pl
from jax.experimental.pallas import tpu as pltpu
from jax.sharding import PartitionSpec as P

F32 = jnp.float32
BF16 = jnp.bfloat16
MESH = pl.DeviceIdType.MESH

DEPTH = 8
ROWS = 4
COLS = 128
HALF = 64
XC = 80
OFFSETS = [
    (dy, dx) for dy in (-2, 2, -1, 1, 0) for dx in (-1, 1, 0) if (dy, dx) != (0, 0)
]
SMALL_LOADS = (1,) + tuple(range(7, 19))
LARGE_LOADS = tuple(range(2, 7))
POOL_PLANE = (0, 2, 1, 3)


def iota(shape, dim):
    return lax.broadcasted_iota(jnp.int32, shape, dim)


def dot(a, b):
    return jnp.dot(a, b, preferred_element_type=F32)


def dot_nt(a, b):
    return lax.dot_general(a, b, (((1,), (1,)), ((), ())), preferred_element_type=F32)


def eye(n):
    return (iota((n, n), 0) == iota((n, n), 1)).astype(BF16)


def repeat_matrix(n, total, dtype):
    return (iota((n, total), 0) == (iota((n, total), 1) & (n - 1))).astype(dtype)


def bands(width, taps):
    count = 128 // width
    lane = iota(taps[0].shape, 1)
    places = [((lane >> (width.bit_length() - 1)) == p).astype(BF16) for p in range(count)]
    placed = [[tap.astype(BF16) * place for place in places] for tap in taps]
    blocks = {}
    for first in range(-1, count + 1):
        terms = [
            placed[dz][first + 1 - dz] for dz in range(3) if 0 <= first + 1 - dz < count
        ]
        blocks[first] = functools.reduce(jnp.add, terms)
    return blocks


def kernel(
    n_wide,
    n_narrow,
    volume,
    w_enter,
    w_encode,
    w_widen,
    w_deep,
    w_upward,
    w_decode,
    w_classes,
    gain_enter,
    shift_enter,
    gain_encode,
    shift_encode,
    gain_widen,
    shift_widen,
    gain_deep,
    shift_deep,
    gain_decode,
    shift_decode,
    bias,
    out,
    v_volume,
    v_enter,
    v_encode,
    v_widen,
    v_deep,
    v_upward,
    v_decode,
    v_classes,
    v_gain_enter,
    v_shift_enter,
    v_gain_encode,
    v_shift_encode,
    v_gain_widen,
    v_shift_widen,
    v_gain_deep,
    v_shift_deep,
    v_gain_decode,
    v_shift_decode,
    s_bias,
    plane_rows,
    own,
    halo,
    m_enter,
    m_encode,
    m_widen,
    m_deep,
    m_upward,
    m_decode,
    m_classes,
    fine,
    coarse,
    first,
    skip,
    pooled,
    widened,
    lifted,
    decoded,
    load_sem,
    send_sem,
    recv_sem,
):
    w = lax.axis_index("wide")
    n = lax.axis_index("narrow")

    def within(at, count):
        return jnp.logical_and(at >= 0, at < count)

    def has(dy, dx):
        return jnp.logical_and(within(w + dy, n_wide), within(n + dx, n_narrow))

    halo[...] = jnp.zeros(halo.shape, BF16)

    barrier = pltpu.get_barrier_semaphore()
    for dy, dx in OFFSETS:

        @pl.when(has(dy, dx))
        def _():
            pl.semaphore_signal(
                barrier, inc=1, device_id=(w + dy, n + dx), device_id_type=MESH
            )

    sources = (
        volume, w_enter, w_encode, w_widen, w_deep, w_upward, w_decode, w_classes,
        gain_enter, shift_enter, gain_encode, shift_encode, gain_widen, shift_widen,
        gain_deep, shift_deep, gain_decode, shift_decode, bias,
    )
    targets = (
        v_volume, v_enter, v_encode, v_widen, v_deep, v_upward, v_decode, v_classes,
        v_gain_enter, v_shift_enter, v_gain_encode, v_shift_encode, v_gain_widen, v_shift_widen,
        v_gain_deep, v_shift_deep, v_gain_decode, v_shift_decode, s_bias,
    )
    loads = [
        pltpu.make_async_copy(source, target, load_sem.at[k])
        for k, (source, target) in enumerate(zip(sources, targets))
    ]
    for load in loads:
        load.start()

    loads[0].wait()
    for z in range(DEPTH):
        plane_rows[ROWS * z : ROWS * (z + 1), :] = v_volume[z].astype(F32)
    by_row = jnp.concatenate(
        [plane_rows[pl.ds(y, DEPTH, stride=ROWS), :] for y in range(ROWS)], axis=0
    )
    by_row = pltpu.roll(by_row, HALF, 1).astype(BF16)
    own[...] = by_row
    halo[1, 64:96, :] = by_row

    def exchange(k):
        dy, dx = OFFSETS[k]
        return pltpu.make_async_remote_copy(
            src_ref=own,
            dst_ref=halo.at[1 - dx, pl.ds(32 * (2 - dy), 32)],
            send_sem=send_sem.at[k],
            recv_sem=recv_sem.at[k],
            device_id=(w + dy, n + dx),
            device_id_type=MESH,
        )

    pl.semaphore_wait(barrier, sum(has(dy, dx).astype(jnp.int32) for dy, dx in OFFSETS))
    for k, (dy, dx) in enumerate(OFFSETS):

        @pl.when(has(dy, dx))
        def _():
            exchange(k).start()

    for k in SMALL_LOADS:
        loads[k].wait()

    def rows_of(refs):
        return jnp.concatenate([ref[...].reshape(1, ref.shape[0]) for ref in refs], axis=0)

    fine[...] = jnp.dot(
        rows_of((v_gain_enter, v_shift_enter, v_gain_encode, v_shift_encode, v_gain_decode, v_shift_decode)),
        repeat_matrix(32, 256, F32),
        preferred_element_type=F32,
        precision=lax.Precision.HIGHEST,
    )
    coarse[...] = jnp.dot(
        rows_of((v_gain_widen, v_shift_widen, v_gain_deep, v_shift_deep)),
        repeat_matrix(64, 256, F32),
        preferred_element_type=F32,
        precision=lax.Precision.HIGHEST,
    )

    taps = dot(v_enter[...], repeat_matrix(32, 256, BF16))
    offset_of = iota((DEPTH, 256), 0) - (iota((DEPTH, 256), 1) >> 5) + 1
    zero = jnp.zeros((DEPTH, 256), F32)
    blocks = {}
    for dx in range(3):
        for dy in range(3):
            block = zero
            for dz in range(3):
                row = 9 * dz + 3 * dy + dx
                block = jnp.where(
                    offset_of == dz, jnp.broadcast_to(taps[row : row + 1], (DEPTH, 256)), block
                )
            blocks[dx, dy] = block
    for yo in range(5):
        for px in range(2):
            pieces = [
                blocks.get((s - px, yin - yo), zero) for s in range(4) for yin in range(8)
            ]
            m_enter[yo, px] = jnp.concatenate(pieces, axis=0).astype(BF16)

    classes = dot(v_classes[...], repeat_matrix(32, 256, BF16))
    at_row = iota((64, 256), 0)
    at_lane = iota((64, 256), 1)
    per_class = jnp.where(
        at_row < 32,
        jnp.broadcast_to(classes[0:1], (64, 256)),
        jnp.broadcast_to(classes[1:2], (64, 256)),
    )
    per_plane = jnp.where(((at_row & 31) >> 2) == (at_lane >> 5), per_class, 0.0)
    for y in range(ROWS):
        m_classes[:, 256 * y : 256 * (y + 1)] = jnp.where(
            (at_row & 3) == y, per_plane, 0.0
        ).astype(BF16)

    for k in LARGE_LOADS:
        loads[k].wait()

    repeat64 = repeat_matrix(64, 128, BF16)
    lane64 = iota((64, 128), 1)
    zero32 = jnp.zeros((32, 128), BF16)
    zero64 = jnp.zeros((64, 128), BF16)

    eye256 = eye(256)

    def turn_taps(ref):
        channels = ref.shape[2]
        count = 256 // channels
        turned = []
        for start in range(0, 27, count):
            row = jnp.concatenate(
                [ref[min(start + k, 26)] for k in range(count)], axis=1
            )
            result = dot_nt(
                eye256, jnp.concatenate([row] * (128 // ref.shape[1]), axis=0)
            ).astype(BF16)
            turned += [result[channels * k : channels * (k + 1)] for k in range(count)]
        return turned

    from_encode = turn_taps(v_encode)
    from_decode = turn_taps(v_decode)
    for tap in range(9):
        blocks = bands(32, [from_encode[9 * dz + tap] for dz in range(3)])
        for z in range(DEPTH):
            for tile in range(2):
                m_encode[tap, 32 * z : 32 * (z + 1), 128 * tile : 128 * (tile + 1)] = (
                    blocks.get(z - 4 * tile, zero32)
                )
        for source in range(2):
            blocks = bands(
                32,
                [from_decode[9 * dz + tap][32 * source : 32 * (source + 1)] for dz in range(3)],
            )
            for z in range(DEPTH):
                for tile in range(2):
                    m_decode[
                        source, tap, 32 * z : 32 * (z + 1), 128 * tile : 128 * (tile + 1)
                    ] = blocks.get(z - 4 * tile, zero32)

    from_widen = dot(v_widen[...].reshape(27 * 32, 64), repeat64).astype(BF16)
    from_deep = turn_taps(v_deep)
    for tap in range(9):
        starts = [32 * (9 * dz + tap) for dz in range(3)]
        blocks = bands(64, [from_widen[start : start + 32] for start in starts])
        for group in range(4):
            for tile in range(2):
                m_widen[
                    tap, 32 * group : 32 * (group + 1), 128 * tile : 128 * (tile + 1)
                ] = blocks.get(POOL_PLANE[group] - 2 * tile, zero32)
        blocks = bands(64, [from_deep[9 * dz + tap] for dz in range(3)])
        for z in range(4):
            for tile in range(2):
                m_deep[tap, 64 * z : 64 * (z + 1), 128 * tile : 128 * (tile + 1)] = (
                    blocks.get(z - 2 * tile, zero64)
                )

    rows = [
        jnp.concatenate([v_upward[4 * a + tap] for tap in range(4)], axis=1) for a in range(2)
    ]
    turned = dot_nt(eye256, jnp.concatenate(rows + rows, axis=0)).astype(BF16)
    halves = [((lane64 >> 6) == half).astype(BF16) for half in range(2)]
    for tap in range(4):
        block = turned[64 * tap : 64 * (tap + 1)]
        for z in range(4):
            for tile in range(2):
                m_upward[tap, 64 * z : 64 * (z + 1), 128 * tile : 128 * (tile + 1)] = (
                    block * halves[z - 2 * tile] if 0 <= z - 2 * tile < 2 else zero64
                )

    def inside(at, count):
        return within(at, count).astype(F32)

    left = inside(n - 1, n_narrow)
    right = inside(n + 1, n_narrow)

    def relu_inside(acc, gain, shift, keep):
        gain = gain * keep
        shift = shift * keep
        return jnp.concatenate(
            [
                jnp.maximum(acc[0:64] * gain + shift, 0.0),
                jnp.maximum(acc[64:72] * (gain * right) + shift * right, 0.0),
                jnp.maximum(acc[72:80] * (gain * left) + shift * left, 0.0),
            ],
            axis=0,
        )

    def put_columns(ref, row, parity, value):
        ref[(1 + parity, *row)] = value.astype(BF16)
        if parity == 0:
            ref[(3, *row)] = pltpu.roll(value, XC - 1, 0).astype(BF16)
        else:
            ref[(0, *row)] = pltpu.roll(value, 1, 0).astype(BF16)

    lane = iota((96, 128), 1)
    at = iota((XC, 256), 0)
    pick = (
        iota((XC, 256), 1) == 2 * jnp.where(at < 72, at, at - XC) + HALF
    ).astype(BF16)
    pool_lane = (iota((XC, 128), 1) & 32) == 0
    encode_matrix = m_encode[...].reshape(9 * 256, 256)
    near = jnp.where(lax.rem(w, 4) < 2, 1, 0)

    for turn in range(2):
        half = near if turn == 0 else 1 - near
        for k, (dy, dx) in enumerate(OFFSETS):
            first_half = 1 if dy < 0 else 0
            if dy == 0:
                now = turn == 0
            else:
                now = near == first_half if turn == 0 else near != first_half

            @pl.when(jnp.logical_and(has(-dy, -dx), now))
            def _():
                exchange(k).wait_recv()

        rows = pl.ds(pl.multiple_of(64 * half, 64), 96)
        before, middle, after = [halo[side, rows, :].astype(F32) for side in range(3)]
        wide_rows = jnp.concatenate(
            [jnp.where(lane < HALF, before, middle), jnp.where(lane < HALF, middle, after)],
            axis=1,
        )
        wide_rows = jnp.concatenate([wide_rows, jnp.zeros((8, 256), F32)], axis=0)
        shifted = [
            wide_rows if s == 1 else pltpu.roll(wide_rows, (1 - s) % 256, 1) for s in range(4)
        ]
        columns = jnp.concatenate(
            [
                dot_nt(
                    pick,
                    jnp.concatenate(
                        [piece[40 * g : 40 * g + 64] for piece in shifted], axis=0
                    ).astype(BF16),
                ).astype(BF16)
                for g in range(2)
            ],
            axis=0,
        )

        for yo in range(5):
            for px in range(2):
                acc = dot(columns, m_enter[yo, px])
                for g in range(2):
                    row = 5 * g + yo
                    keep = inside(w * ROWS - 7 + 8 * half + row, n_wide * ROWS)
                    put_columns(
                        first, (turn, row), px,
                        relu_inside(
                            acc[XC * g : XC * (g + 1)], fine[0:1, :], fine[1:2, :], keep
                        ),
                    )

        parity_acc = []
        for px in range(2):
            pieces = [
                first[px + dx, turn, dy : dy + 8].reshape(8 * XC, 256)
                for dy in range(3)
                for dx in range(3)
            ]
            parity_acc.append(dot(jnp.concatenate(pieces, axis=1), encode_matrix))
        for k in range(4):
            keep = inside(w * 2 - 3 + 4 * half + k, n_wide * 2)
            best = None
            for y in range(2):
                row = 2 * k + y
                for px in range(2):
                    value = relu_inside(
                        parity_acc[px][XC * row : XC * (row + 1)],
                        fine[2:3, :], fine[3:4, :], keep,
                    )
                    if row not in (3, 4):
                        put_columns(skip, (8 * half + row,), px, value)
                    best = value if best is None else jnp.maximum(best, value)
            low = best[:, 0:128]
            high = best[:, 128:256]
            low = jnp.maximum(low, pltpu.roll(low, 96, 1))
            high = jnp.maximum(high, pltpu.roll(high, 96, 1))
            best = jnp.where(pool_lane, low, pltpu.roll(high, 32, 1))
            pooled[0, 4 * half + k] = pltpu.roll(best, 1, 0).astype(BF16)
            pooled[1, 4 * half + k] = best.astype(BF16)
            pooled[2, 4 * half + k] = pltpu.roll(best, XC - 1, 0).astype(BF16)

    pieces = [
        pooled[dx, dy : dy + 6].reshape(6 * XC, 128) for dy in range(3) for dx in range(3)
    ]
    acc = dot(jnp.concatenate(pieces, axis=1), m_widen[...].reshape(9 * 128, 256))
    for k in range(6):
        keep = inside(w * 2 - 2 + k, n_wide * 2)
        value = relu_inside(acc[XC * k : XC * (k + 1)], coarse[0:1, :], coarse[1:2, :], keep)
        widened[0, k] = pltpu.roll(value, 1, 0).astype(BF16)
        widened[1, k] = value.astype(BF16)
        widened[2, k] = pltpu.roll(value, XC - 1, 0).astype(BF16)

    pieces = [
        widened[dx, dy : dy + 4].reshape(4 * XC, 256) for dy in range(3) for dx in range(3)
    ]
    acc = dot(jnp.concatenate(pieces, axis=1), m_deep[...].reshape(9 * 256, 256))
    deepest = jnp.concatenate(
        [
            relu_inside(
                acc[XC * k : XC * (k + 1)],
                coarse[2:3, :],
                coarse[3:4, :],
                inside(w * 2 - 1 + k, n_wide * 2),
            )
            for k in range(4)
        ],
        axis=0,
    ).astype(BF16)

    for b in range(2):
        source = deepest[XC * (1 - b) : XC * (4 - b)]
        for e in range(2):
            acc = dot(source, m_upward[2 * b + e])
            for k in range(3):
                put_columns(lifted, (2 * k + 1 - b,), e, acc[XC * k : XC * (k + 1)])

    accs = []
    for px in range(2):
        pieces = [
            ref[px + dx, start + dy : start + dy + ROWS, 0:HALF].reshape(ROWS * HALF, 256)
            for ref, start in ((skip, 5), (lifted, 0))
            for dy in range(3)
            for dx in range(3)
        ]
        accs.append(dot(jnp.concatenate(pieces, axis=1), m_decode[...].reshape(18 * 256, 256)))
    acc = jnp.concatenate(accs, axis=0)
    value = jnp.maximum(acc * fine[4:5, :] + fine[5:6, :], 0.0)
    for px in range(2):
        for y in range(ROWS):
            start = (px * ROWS + y) * HALF
            for tile in range(2):
                decoded[tile, pl.ds(y * COLS + px, HALF, stride=2), :] = value[
                    start : start + HALF, 128 * tile : 128 * (tile + 1)
                ]

    features = jnp.concatenate(
        [
            decoded[tile, y * COLS : (y + 1) * COLS, :].astype(BF16)
            for y in range(ROWS)
            for tile in range(2)
        ],
        axis=1,
    )
    logits = dot_nt(m_classes[...], features)
    for k, (dy, dx) in enumerate(OFFSETS):

        @pl.when(has(dy, dx))
        def _():
            exchange(k).wait_send()

    out[...] = logits + jnp.where(iota((64, 128), 0) < 32, s_bias[0], s_bias[1])


def per_device(
    n_wide,
    n_narrow,
    volume,
    w_enter,
    gain_enter,
    shift_enter,
    w_encode,
    gain_encode,
    shift_encode,
    w_widen,
    gain_widen,
    shift_widen,
    w_deep,
    gain_deep,
    shift_deep,
    w_upward,
    w_decode,
    gain_decode,
    shift_decode,
    w_classes,
    bias_classes,
):
    operands = (
        volume.reshape(DEPTH, ROWS, COLS),
        w_enter.reshape(27, 32),
        w_encode,
        jnp.transpose(w_widen, (0, 2, 1)),
        w_deep,
        w_upward,
        w_decode,
        w_classes,
        gain_enter,
        shift_enter,
        gain_encode,
        shift_encode,
        gain_widen,
        shift_widen,
        gain_deep,
        shift_deep,
        gain_decode,
        shift_decode,
        bias_classes,
    )
    copies = [pltpu.VMEM(x.shape, x.dtype) for x in operands[:-1]]
    copies.append(pltpu.SMEM((2,), F32))
    logits = pl.pallas_call(
        functools.partial(kernel, n_wide, n_narrow),
        out_shape=jax.ShapeDtypeStruct((64, COLS), F32),
        in_specs=[pl.BlockSpec(memory_space=pltpu.HBM)] * len(operands),
        out_specs=pl.BlockSpec(memory_space=pltpu.VMEM),
        scratch_shapes=copies
        + [
            pltpu.VMEM((32, COLS), F32),
            pltpu.VMEM((32, COLS), BF16),
            pltpu.VMEM((3, 160, COLS), BF16),
            pltpu.VMEM((5, 2, 256, 256), BF16),
            pltpu.VMEM((9, 256, 256), BF16),
            pltpu.VMEM((9, 128, 256), BF16),
            pltpu.VMEM((9, 256, 256), BF16),
            pltpu.VMEM((4, 256, 256), BF16),
            pltpu.VMEM((2, 9, 256, 256), BF16),
            pltpu.VMEM((64, 1024), BF16),
            pltpu.VMEM((6, 256), F32),
            pltpu.VMEM((4, 256), F32),
            pltpu.VMEM((4, 2, 10, XC, 256), BF16),
            pltpu.VMEM((4, 16, XC, 256), BF16),
            pltpu.VMEM((3, 8, XC, 128), BF16),
            pltpu.VMEM((3, 6, XC, 256), BF16),
            pltpu.VMEM((4, 6, XC, 256), BF16),
            pltpu.VMEM((2, ROWS * COLS, 128), F32),
            pltpu.SemaphoreType.DMA((len(operands),)),
            pltpu.SemaphoreType.DMA((len(OFFSETS),)),
            pltpu.SemaphoreType.DMA((len(OFFSETS),)),
        ],
        compiler_params=pltpu.CompilerParams(
            collective_id=0, has_side_effects=True, vmem_limit_bytes=52 * 1024 * 1024
        ),
        name="unet",
    )(*[pltpu.with_memory_space_constraint(x, pltpu.HBM) for x in operands])
    return logits.reshape(2, DEPTH, ROWS, COLS)


def solution(mesh):
    in_specs = (P(None, None, "wide", "narrow"),) + (P(),) * 18
    return jax.shard_map(
        functools.partial(per_device, mesh.shape["wide"], mesh.shape["narrow"]),
        mesh=mesh,
        in_specs=in_specs,
        out_specs=P(None, None, "wide", "narrow"),
        check_vma=False,
    )
```

```python
import functools

import jax
import jax.numpy as jnp
from jax import lax
from jax.experimental import pallas as pl
from jax.experimental.pallas import tpu as pltpu
from jax.sharding import PartitionSpec as P

F32 = jnp.float32
BF16 = jnp.bfloat16
MESH = pl.DeviceIdType.MESH

DEPTH = 8
ROWS = 4
COLS = 128
HALF = 64
XC = 80
OFFSETS = [
    (dy, dx) for dy in (-2, 2, -1, 1, 0) for dx in (-1, 1, 0) if (dy, dx) != (0, 0)
]
SMALL_LOADS = (1,) + tuple(range(7, 19))
LARGE_LOADS = tuple(range(2, 7))
POOL_PLANE = (0, 2, 1, 3)


def iota(shape, dim):
    return lax.broadcasted_iota(jnp.int32, shape, dim)


def dot(a, b):
    return jnp.dot(a, b, preferred_element_type=F32)


def dot_nt(a, b):
    return lax.dot_general(a, b, (((1,), (1,)), ((), ())), preferred_element_type=F32)


def eye(n):
    return (iota((n, n), 0) == iota((n, n), 1)).astype(BF16)


def repeat_matrix(n, total, dtype):
    return (iota((n, total), 0) == (iota((n, total), 1) & (n - 1))).astype(dtype)


def bands(width, taps):
    count = 128 // width
    lane = iota(taps[0].shape, 1)
    places = [((lane >> (width.bit_length() - 1)) == p).astype(BF16) for p in range(count)]
    placed = [[tap.astype(BF16) * place for place in places] for tap in taps]
    blocks = {}
    for first in range(-1, count + 1):
        terms = [
            placed[dz][first + 1 - dz] for dz in range(3) if 0 <= first + 1 - dz < count
        ]
        blocks[first] = functools.reduce(jnp.add, terms)
    return blocks


def kernel(
    n_wide,
    n_narrow,
    volume,
    w_enter,
    w_encode,
    w_widen,
    w_deep,
    w_upward,
    w_decode,
    w_classes,
    gain_enter,
    shift_enter,
    gain_encode,
    shift_encode,
    gain_widen,
    shift_widen,
    gain_deep,
    shift_deep,
    gain_decode,
    shift_decode,
    bias,
    out,
    v_volume,
    v_enter,
    v_encode,
    v_widen,
    v_deep,
    v_upward,
    v_decode,
    v_classes,
    v_gain_enter,
    v_shift_enter,
    v_gain_encode,
    v_shift_encode,
    v_gain_widen,
    v_shift_widen,
    v_gain_deep,
    v_shift_deep,
    v_gain_decode,
    v_shift_decode,
    s_bias,
    plane_rows,
    own,
    own_edge,
    halo,
    edges,
    m_enter,
    m_encode,
    m_widen,
    m_deep,
    m_upward,
    m_decode,
    m_classes,
    fine,
    coarse,
    first,
    skip,
    pooled,
    widened,
    lifted,
    decoded,
    load_sem,
    send_sem,
    recv_sem,
):
    w = lax.axis_index("wide")
    n = lax.axis_index("narrow")

    def within(at, count):
        return jnp.logical_and(at >= 0, at < count)

    def has(dy, dx):
        return jnp.logical_and(within(w + dy, n_wide), within(n + dx, n_narrow))

    halo[...] = jnp.zeros(halo.shape, BF16)
    edges[...] = jnp.zeros(edges.shape, BF16)

    barrier = pltpu.get_barrier_semaphore()
    for dy, dx in OFFSETS:

        @pl.when(has(dy, dx))
        def _():
            pl.semaphore_signal(
                barrier, inc=1, device_id=(w + dy, n + dx), device_id_type=MESH
            )

    sources = (
        volume, w_enter, w_encode, w_widen, w_deep, w_upward, w_decode, w_classes,
        gain_enter, shift_enter, gain_encode, shift_encode, gain_widen, shift_widen,
        gain_deep, shift_deep, gain_decode, shift_decode, bias,
    )
    targets = (
        v_volume, v_enter, v_encode, v_widen, v_deep, v_upward, v_decode, v_classes,
        v_gain_enter, v_shift_enter, v_gain_encode, v_shift_encode, v_gain_widen, v_shift_widen,
        v_gain_deep, v_shift_deep, v_gain_decode, v_shift_decode, s_bias,
    )
    loads = [
        pltpu.make_async_copy(source, target, load_sem.at[k])
        for k, (source, target) in enumerate(zip(sources, targets))
    ]
    for load in loads:
        load.start()

    loads[0].wait()
    for z in range(DEPTH):
        plane_rows[ROWS * z : ROWS * (z + 1), :] = v_volume[z].astype(F32)
    by_row = jnp.concatenate(
        [plane_rows[pl.ds(y, DEPTH, stride=ROWS), :] for y in range(ROWS)], axis=0
    )
    by_row = pltpu.roll(by_row, HALF, 1)
    own[...] = by_row.astype(BF16)
    halo[64:96, :] = by_row.astype(BF16)
    own_edge[...] = jnp.where(
        iota((16, COLS), 1) < 80, by_row[0:16], pltpu.roll(by_row[16:32], 32, 1)
    ).astype(BF16)

    def exchange(k):
        dy, dx = OFFSETS[k]
        if dx == 0:
            source, target = own, halo.at[pl.ds(32 * (2 - dy), 32)]
        else:
            source, target = own_edge, edges.at[(1 - dx) // 2, pl.ds(16 * (2 - dy), 16)]
        return pltpu.make_async_remote_copy(
            src_ref=source,
            dst_ref=target,
            send_sem=send_sem.at[k],
            recv_sem=recv_sem.at[k],
            device_id=(w + dy, n + dx),
            device_id_type=MESH,
        )

    pl.semaphore_wait(barrier, sum(has(dy, dx).astype(jnp.int32) for dy, dx in OFFSETS))
    for k, (dy, dx) in enumerate(OFFSETS):

        @pl.when(has(dy, dx))
        def _():
            exchange(k).start()

    for k in SMALL_LOADS:
        loads[k].wait()

    def rows_of(refs):
        return jnp.concatenate([ref[...].reshape(1, ref.shape[0]) for ref in refs], axis=0)

    fine[...] = jnp.dot(
        rows_of((v_gain_enter, v_shift_enter, v_gain_encode, v_shift_encode, v_gain_decode, v_shift_decode)),
        repeat_matrix(32, 256, F32),
        preferred_element_type=F32,
        precision=lax.Precision.HIGHEST,
    )
    coarse[...] = jnp.dot(
        rows_of((v_gain_widen, v_shift_widen, v_gain_deep, v_shift_deep)),
        repeat_matrix(64, 256, F32),
        preferred_element_type=F32,
        precision=lax.Precision.HIGHEST,
    )

    taps = dot(v_enter[...], repeat_matrix(32, 256, BF16))
    offset_of = iota((DEPTH, 256), 0) - (iota((DEPTH, 256), 1) >> 5) + 1
    zero = jnp.zeros((DEPTH, 256), F32)
    blocks = {}
    for dx in range(3):
        for dy in range(3):
            block = zero
            for dz in range(3):
                row = 9 * dz + 3 * dy + dx
                block = jnp.where(
                    offset_of == dz, jnp.broadcast_to(taps[row : row + 1], (DEPTH, 256)), block
                )
            blocks[dx, dy] = block
    for yo in range(5):
        for px in range(2):
            pieces = [
                blocks.get((s - px, yin - yo), zero) for s in range(4) for yin in range(8)
            ]
            m_enter[yo, px] = jnp.concatenate(pieces, axis=0).astype(BF16)

    classes = dot(v_classes[...], repeat_matrix(32, 256, BF16))
    at_row = iota((64, 256), 0)
    at_lane = iota((64, 256), 1)
    per_class = jnp.where(
        at_row < 32,
        jnp.broadcast_to(classes[0:1], (64, 256)),
        jnp.broadcast_to(classes[1:2], (64, 256)),
    )
    per_plane = jnp.where(((at_row & 31) >> 2) == (at_lane >> 5), per_class, 0.0)
    for y in range(ROWS):
        m_classes[:, 256 * y : 256 * (y + 1)] = jnp.where(
            (at_row & 3) == y, per_plane, 0.0
        ).astype(BF16)

    for k in LARGE_LOADS:
        loads[k].wait()

    repeat64 = repeat_matrix(64, 128, BF16)
    lane64 = iota((64, 128), 1)
    zero32 = jnp.zeros((32, 128), BF16)
    zero64 = jnp.zeros((64, 128), BF16)

    eye256 = eye(256)

    def turn_taps(ref):
        channels = ref.shape[2]
        count = 256 // channels
        turned = []
        for start in range(0, 27, count):
            row = jnp.concatenate(
                [ref[min(start + k, 26)] for k in range(count)], axis=1
            )
            result = dot_nt(
                eye256, jnp.concatenate([row] * (128 // ref.shape[1]), axis=0)
            ).astype(BF16)
            turned += [result[channels * k : channels * (k + 1)] for k in range(count)]
        return turned

    from_encode = turn_taps(v_encode)
    from_decode = turn_taps(v_decode)
    for tap in range(9):
        blocks = bands(32, [from_encode[9 * dz + tap] for dz in range(3)])
        for z in range(DEPTH):
            for tile in range(2):
                m_encode[tap, 32 * z : 32 * (z + 1), 128 * tile : 128 * (tile + 1)] = (
                    blocks.get(z - 4 * tile, zero32)
                )
        for source in range(2):
            blocks = bands(
                32,
                [from_decode[9 * dz + tap][32 * source : 32 * (source + 1)] for dz in range(3)],
            )
            for z in range(DEPTH):
                for tile in range(2):
                    m_decode[
                        source, tap, 32 * z : 32 * (z + 1), 128 * tile : 128 * (tile + 1)
                    ] = blocks.get(z - 4 * tile, zero32)

    from_widen = dot(v_widen[...].reshape(27 * 32, 64), repeat64).astype(BF16)
    from_deep = turn_taps(v_deep)
    for tap in range(9):
        starts = [32 * (9 * dz + tap) for dz in range(3)]
        blocks = bands(64, [from_widen[start : start + 32] for start in starts])
        for group in range(4):
            for tile in range(2):
                m_widen[
                    tap, 32 * group : 32 * (group + 1), 128 * tile : 128 * (tile + 1)
                ] = blocks.get(POOL_PLANE[group] - 2 * tile, zero32)
        blocks = bands(64, [from_deep[9 * dz + tap] for dz in range(3)])
        for z in range(4):
            for tile in range(2):
                m_deep[tap, 64 * z : 64 * (z + 1), 128 * tile : 128 * (tile + 1)] = (
                    blocks.get(z - 2 * tile, zero64)
                )

    rows = [
        jnp.concatenate([v_upward[4 * a + tap] for tap in range(4)], axis=1) for a in range(2)
    ]
    turned = dot_nt(eye256, jnp.concatenate(rows + rows, axis=0)).astype(BF16)
    halves = [((lane64 >> 6) == half).astype(BF16) for half in range(2)]
    for tap in range(4):
        block = turned[64 * tap : 64 * (tap + 1)]
        for z in range(4):
            for tile in range(2):
                m_upward[tap, 64 * z : 64 * (z + 1), 128 * tile : 128 * (tile + 1)] = (
                    block * halves[z - 2 * tile] if 0 <= z - 2 * tile < 2 else zero64
                )

    def inside(at, count):
        return within(at, count).astype(F32)

    left = inside(n - 1, n_narrow)
    right = inside(n + 1, n_narrow)

    def relu_inside(acc, gain, shift, keep):
        gain = gain * keep
        shift = shift * keep
        return jnp.concatenate(
            [
                jnp.maximum(acc[0:64] * gain + shift, 0.0),
                jnp.maximum(acc[64:72] * (gain * right) + shift * right, 0.0),
                jnp.maximum(acc[72:80] * (gain * left) + shift * left, 0.0),
            ],
            axis=0,
        )

    def put_columns(ref, row, parity, value):
        ref[(1 + parity, *row)] = value.astype(BF16)
        if parity == 0:
            ref[(3, *row)] = pltpu.roll(value, XC - 1, 0).astype(BF16)
        else:
            ref[(0, *row)] = pltpu.roll(value, 1, 0).astype(BF16)

    lane = iota((96, 128), 1)
    at = iota((XC, 256), 0)
    pick = (
        iota((XC, 256), 1) == 2 * jnp.where(at < 72, at, at - XC) + HALF
    ).astype(BF16)
    pool_lane = (iota((XC, 128), 1) & 32) == 0
    encode_matrix = m_encode[...].reshape(9 * 256, 256)
    near = jnp.where(lax.rem(w, 4) < 2, 1, 0)

    for turn in range(2):
        half = near if turn == 0 else 1 - near
        for k, (dy, dx) in enumerate(OFFSETS):
            first_half = 1 if dy < 0 else 0
            if dy == 0:
                now = turn == 0
            else:
                now = near == first_half if turn == 0 else near != first_half

            @pl.when(jnp.logical_and(has(-dy, -dx), now))
            def _():
                exchange(k).wait_recv()

        rows = pl.ds(pl.multiple_of(64 * half, 64), 96)
        middle = halo[rows, :].astype(F32)
        rows = pl.ds(pl.multiple_of(32 * half, 32), 48)
        sides = []
        for side in range(2):
            packed = edges[side, rows, :].astype(F32)
            pieces = []
            for block in range(3):
                piece = packed[16 * block : 16 * (block + 1)]
                pieces += [piece, pltpu.roll(piece, 96, 1)]
            sides.append(jnp.concatenate(pieces, axis=0))
        before, after = sides
        wide_rows = jnp.concatenate(
            [jnp.where(lane < HALF, before, middle), jnp.where(lane < HALF, middle, after)],
            axis=1,
        )
        wide_rows = jnp.concatenate([wide_rows, jnp.zeros((8, 256), F32)], axis=0)
        shifted = [
            wide_rows if s == 1 else pltpu.roll(wide_rows, (1 - s) % 256, 1) for s in range(4)
        ]
        columns = jnp.concatenate(
            [
                dot_nt(
                    pick,
                    jnp.concatenate(
                        [piece[40 * g : 40 * g + 64] for piece in shifted], axis=0
                    ).astype(BF16),
                ).astype(BF16)
                for g in range(2)
            ],
            axis=0,
        )

        for yo in range(5):
            for px in range(2):
                acc = dot(columns, m_enter[yo, px])
                for g in range(2):
                    row = 5 * g + yo
                    keep = inside(w * ROWS - 7 + 8 * half + row, n_wide * ROWS)
                    put_columns(
                        first, (turn, row), px,
                        relu_inside(
                            acc[XC * g : XC * (g + 1)], fine[0:1, :], fine[1:2, :], keep
                        ),
                    )

        parity_acc = []
        for px in range(2):
            pieces = [
                first[px + dx, turn, dy : dy + 8].reshape(8 * XC, 256)
                for dy in range(3)
                for dx in range(3)
            ]
            parity_acc.append(dot(jnp.concatenate(pieces, axis=1), encode_matrix))
        for k in range(4):
            keep = inside(w * 2 - 3 + 4 * half + k, n_wide * 2)
            best = None
            for y in range(2):
                row = 2 * k + y
                for px in range(2):
                    value = relu_inside(
                        parity_acc[px][XC * row : XC * (row + 1)],
                        fine[2:3, :], fine[3:4, :], keep,
                    )
                    if row not in (3, 4):
                        put_columns(skip, (8 * half + row,), px, value)
                    best = value if best is None else jnp.maximum(best, value)
            low = best[:, 0:128]
            high = best[:, 128:256]
            low = jnp.maximum(low, pltpu.roll(low, 96, 1))
            high = jnp.maximum(high, pltpu.roll(high, 96, 1))
            best = jnp.where(pool_lane, low, pltpu.roll(high, 32, 1))
            pooled[0, 4 * half + k] = pltpu.roll(best, 1, 0).astype(BF16)
            pooled[1, 4 * half + k] = best.astype(BF16)
            pooled[2, 4 * half + k] = pltpu.roll(best, XC - 1, 0).astype(BF16)

    pieces = [
        pooled[dx, dy : dy + 6].reshape(6 * XC, 128) for dy in range(3) for dx in range(3)
    ]
    acc = dot(jnp.concatenate(pieces, axis=1), m_widen[...].reshape(9 * 128, 256))
    for k in range(6):
        keep = inside(w * 2 - 2 + k, n_wide * 2)
        value = relu_inside(acc[XC * k : XC * (k + 1)], coarse[0:1, :], coarse[1:2, :], keep)
        widened[0, k] = pltpu.roll(value, 1, 0).astype(BF16)
        widened[1, k] = value.astype(BF16)
        widened[2, k] = pltpu.roll(value, XC - 1, 0).astype(BF16)

    pieces = [
        widened[dx, dy : dy + 4].reshape(4 * XC, 256) for dy in range(3) for dx in range(3)
    ]
    acc = dot(jnp.concatenate(pieces, axis=1), m_deep[...].reshape(9 * 256, 256))
    deepest = jnp.concatenate(
        [
            relu_inside(
                acc[XC * k : XC * (k + 1)],
                coarse[2:3, :],
                coarse[3:4, :],
                inside(w * 2 - 1 + k, n_wide * 2),
            )
            for k in range(4)
        ],
        axis=0,
    ).astype(BF16)

    for b in range(2):
        source = deepest[XC * (1 - b) : XC * (4 - b)]
        for e in range(2):
            acc = dot(source, m_upward[2 * b + e])
            for k in range(3):
                put_columns(lifted, (2 * k + 1 - b,), e, acc[XC * k : XC * (k + 1)])

    accs = []
    for px in range(2):
        pieces = [
            ref[px + dx, start + dy : start + dy + ROWS, 0:HALF].reshape(ROWS * HALF, 256)
            for ref, start in ((skip, 5), (lifted, 0))
            for dy in range(3)
            for dx in range(3)
        ]
        accs.append(dot(jnp.concatenate(pieces, axis=1), m_decode[...].reshape(18 * 256, 256)))
    acc = jnp.concatenate(accs, axis=0)
    value = jnp.maximum(acc * fine[4:5, :] + fine[5:6, :], 0.0)
    for px in range(2):
        for y in range(ROWS):
            start = (px * ROWS + y) * HALF
            for tile in range(2):
                decoded[tile, pl.ds(y * COLS + px, HALF, stride=2), :] = value[
                    start : start + HALF, 128 * tile : 128 * (tile + 1)
                ]

    features = jnp.concatenate(
        [
            decoded[tile, y * COLS : (y + 1) * COLS, :].astype(BF16)
            for y in range(ROWS)
            for tile in range(2)
        ],
        axis=1,
    )
    logits = dot_nt(m_classes[...], features)
    for k, (dy, dx) in enumerate(OFFSETS):

        @pl.when(has(dy, dx))
        def _():
            exchange(k).wait_send()

    out[...] = logits + jnp.where(iota((64, 128), 0) < 32, s_bias[0], s_bias[1])


def per_device(
    n_wide,
    n_narrow,
    volume,
    w_enter,
    gain_enter,
    shift_enter,
    w_encode,
    gain_encode,
    shift_encode,
    w_widen,
    gain_widen,
    shift_widen,
    w_deep,
    gain_deep,
    shift_deep,
    w_upward,
    w_decode,
    gain_decode,
    shift_decode,
    w_classes,
    bias_classes,
):
    operands = (
        volume.reshape(DEPTH, ROWS, COLS),
        w_enter.reshape(27, 32),
        w_encode,
        jnp.transpose(w_widen, (0, 2, 1)),
        w_deep,
        w_upward,
        w_decode,
        w_classes,
        gain_enter,
        shift_enter,
        gain_encode,
        shift_encode,
        gain_widen,
        shift_widen,
        gain_deep,
        shift_deep,
        gain_decode,
        shift_decode,
        bias_classes,
    )
    copies = [pltpu.VMEM(x.shape, x.dtype) for x in operands[:-1]]
    copies.append(pltpu.SMEM((2,), F32))
    logits = pl.pallas_call(
        functools.partial(kernel, n_wide, n_narrow),
        out_shape=jax.ShapeDtypeStruct((64, COLS), F32),
        in_specs=[pl.BlockSpec(memory_space=pltpu.HBM)] * len(operands),
        out_specs=pl.BlockSpec(memory_space=pltpu.VMEM),
        scratch_shapes=copies
        + [
            pltpu.VMEM((32, COLS), F32),
            pltpu.VMEM((32, COLS), BF16),
            pltpu.VMEM((16, COLS), BF16),
            pltpu.VMEM((160, COLS), BF16),
            pltpu.VMEM((2, 80, COLS), BF16),
            pltpu.VMEM((5, 2, 256, 256), BF16),
            pltpu.VMEM((9, 256, 256), BF16),
            pltpu.VMEM((9, 128, 256), BF16),
            pltpu.VMEM((9, 256, 256), BF16),
            pltpu.VMEM((4, 256, 256), BF16),
            pltpu.VMEM((2, 9, 256, 256), BF16),
            pltpu.VMEM((64, 1024), BF16),
            pltpu.VMEM((6, 256), F32),
            pltpu.VMEM((4, 256), F32),
            pltpu.VMEM((4, 2, 10, XC, 256), BF16),
            pltpu.VMEM((4, 16, XC, 256), BF16),
            pltpu.VMEM((3, 8, XC, 128), BF16),
            pltpu.VMEM((3, 6, XC, 256), BF16),
            pltpu.VMEM((4, 6, XC, 256), BF16),
            pltpu.VMEM((2, ROWS * COLS, 128), F32),
            pltpu.SemaphoreType.DMA((len(operands),)),
            pltpu.SemaphoreType.DMA((len(OFFSETS),)),
            pltpu.SemaphoreType.DMA((len(OFFSETS),)),
        ],
        compiler_params=pltpu.CompilerParams(
            collective_id=0, has_side_effects=True, vmem_limit_bytes=52 * 1024 * 1024
        ),
        name="unet",
    )(*[pltpu.with_memory_space_constraint(x, pltpu.HBM) for x in operands])
    return logits.reshape(2, DEPTH, ROWS, COLS)


def solution(mesh):
    in_specs = (P(None, None, "wide", "narrow"),) + (P(),) * 18
    return jax.shard_map(
        functools.partial(per_device, mesh.shape["wide"], mesh.shape["narrow"]),
        mesh=mesh,
        in_specs=in_specs,
        out_specs=P(None, None, "wide", "narrow"),
        check_vma=False,
    )
```
